512 devices in a mesh: grp: 8 (over y, core), tile: 64 (over z, x).
Axes of the slice: x: 4, y: 4, z: 16, core: 2. Of those that a mesh axis runs over, the one named last changes fastest.
Arguments:
- spectrum: float32 [36, 36, 131072], P(None, None, ('grp', 'tile')), may hold values from 0 to 2
- courant: float32 [36], replicated, may hold values from 0.15 to 0.7
- decay: float32 [36], replicated, may hold values from 0.05 to 0.5
- land: int32 [1024, 128], P('tile', 'grp'), may hold values 0 or 1
- ice_rows: float32 [3, 131072], P(None, ('grp', 'tile')), may hold values from 0 to 1
- ice_route: int32 [2, 131072], P(None, ('grp', 'tile')), may hold values from 0 to 63, as said below
- wave_source: int32 [2, 1024, 128], P(None, 'tile', 'grp'), may hold values from 0 to 63, as said below
Outputs:
- spectrum_out: float32 [36, 36, 131072], P(None, None, ('grp', 'tile'))
- coupling: float32 [4, 131072], P(None, ('grp', 'tile'))
The draws below stay inside these ranges and needn't reach their ends.
Inputs may be any that keep to these rules, and one draw needn't show every extreme that they name: `ice_route`: row 0 is a tile index, row 1 a slot. Within a group, the rows of ice device t with tile index d take slots 0 to n-1 once each, where n is at most 6, equals 6 for exactly one d of every t and 2 for exactly one other. `wave_source`: row 0 is an ice device index within the group, row 1 a slot; the cells of wave device (g, d) hold exactly the pairs (t, s) of the rows of group g that ice_route sends to d, each once.
All inputs are finite; a program needn't handle non-finite values. No bound on the sum of `land` on one device may be relied on, other than what follows from the above.
Results may differ from the reference program's by a relative error of at most 0.00014.
Values sent between devices are 32-bit elements; how exact they have to be, the bound alone decides.
A program may use at most 128 MiB of HBM per device.

```python
import math
import jax
import jax.numpy as jnp
from jax import lax

TH = 36
K = 36
CX = 16
CY = 16
NX = 1024
NY = 128
CELLS = 131072
ROWS = 131072
N_GRP = 8
N_TILE = 64


def route_plan(key):
    groups = N_GRP
    tiles = N_TILE
    count = CX * CY
    base = count // tiles
    kick = base // 2
    key_perm, key_send, key_recv = jax.random.split(key, 3)
    partner = jax.vmap(lambda sub: jax.random.permutation(sub, tiles))(jax.random.split(key_perm, groups))
    columns = jnp.arange(tiles).astype(jnp.int32)
    upper = (columns[None, None, :] == partner[:, :, None]).astype(jnp.int32)
    lower = (columns[None, None, :] == ((partner + 1) % tiles)[:, :, None]).astype(jnp.int32)
    matrix = base + kick * (upper - lower)
    positions = jnp.arange(count).astype(jnp.int32)
    send_cum = jnp.cumsum(matrix, axis=2)
    dest_sorted = jnp.sum((send_cum[:, :, None, :] <= positions[None, None, :, None]).astype(jnp.int32), axis=3)
    send_start = send_cum - matrix
    slot_sorted = positions[None, None, :] - jnp.take_along_axis(send_start, dest_sorted, axis=2)
    shuffle = jax.vmap(lambda sub: jax.random.permutation(sub, count))(jax.random.split(key_send, groups * tiles)).reshape(groups, tiles, count)
    dest = jnp.take_along_axis(dest_sorted, shuffle, axis=2)
    slot = jnp.take_along_axis(slot_sorted, shuffle, axis=2)
    route = jnp.stack([dest, slot]).reshape(2, groups * tiles * count).astype(jnp.int32)
    matrix_in = jnp.transpose(matrix, (0, 2, 1))
    recv_cum = jnp.cumsum(matrix_in, axis=2)
    src_sorted = jnp.sum((recv_cum[:, :, None, :] <= positions[None, None, :, None]).astype(jnp.int32), axis=3)
    recv_start = recv_cum - matrix_in
    rslot_sorted = positions[None, None, :] - jnp.take_along_axis(recv_start, src_sorted, axis=2)
    reshuffle = jax.vmap(lambda sub: jax.random.permutation(sub, count))(jax.random.split(key_recv, groups * tiles)).reshape(groups, tiles, count)
    source = jnp.take_along_axis(src_sorted, reshuffle, axis=2)
    source_slot = jnp.take_along_axis(rslot_sorted, reshuffle, axis=2)
    stacked = jnp.stack([source, source_slot]).reshape(2, groups, tiles, CX, CY)
    wave = jnp.transpose(stacked, (0, 2, 3, 1, 4)).reshape(2, NX, NY).astype(jnp.int32)
    return (route, wave)


def draw_ice_route(key, part):
    return route_plan(key)[0]


def draw_wave_source(key, part):
    return route_plan(key)[1]


def plant(entries, own_key, low, largest):
    spot = [jax.random.randint(jax.random.fold_in(own_key, axis), (), 0, length) for axis, length in enumerate(entries.shape)]
    main_axis = entries.shape.index(max(entries.shape))
    neighbour = spot[:main_axis] + [(spot[main_axis] + 1) % entries.shape[main_axis]] + spot[main_axis + 1:]
    return entries.at[tuple(spot)].set(low).at[tuple(neighbour)].set(largest)


def block_scale(stream_key, dims, cuts, least, high):
    loudness = 1.0
    for dim, blocks in cuts:
        draws = jax.random.uniform(jax.random.fold_in(jax.random.fold_in(stream_key, 6), dim), (blocks,), jnp.float32, least / len(cuts), high / len(cuts))
        loudness = loudness * jnp.repeat(jnp.exp(draws), dims[dim] // blocks).reshape((-1,) + (1,) * (len(dims) - 1 - dim))
    return loudness


def setup_inputs(seed: int = 0) -> dict:
    splits = jax.random.split(jax.random.key(seed), 8)
    spectrum = jnp.clip(2.0 * jax.random.uniform(splits[0], (TH, K, CELLS), jnp.float32) ** block_scale(splits[0], (TH, K, CELLS), ((2, 512),), -0.2, 0.2), 0.0, 2.0)
    courant = jnp.clip(jnp.exp(jax.random.uniform(splits[1], (K,), jnp.float32, math.log(0.15), math.log(0.7))), 0.15, 0.7)
    decay = jnp.clip(jnp.exp(jax.random.uniform(splits[2], (K,), jnp.float32, math.log(0.05), math.log(0.5))), 0.05, 0.5)
    land = plant((jax.random.randint(splits[3], (NX, NY), 0, 10) < 9).astype(jnp.int32), jax.random.fold_in(splits[3], 1), 0, 1)
    ice_rows = jnp.clip(1.0 * jax.random.uniform(splits[4], (3, ROWS), jnp.float32) ** block_scale(splits[4], (3, ROWS), ((1, 512),), -0.2, 0.2), 0.0, 1.0)
    ice_route = draw_ice_route(jax.random.fold_in(splits[7], 71), 0)
    wave_source = draw_wave_source(jax.random.fold_in(splits[7], 71), 0)
    return {"spectrum": spectrum, "courant": courant, "decay": decay, "land": land, "ice_rows": ice_rows, "ice_route": ice_route, "wave_source": wave_source}


def advect(padded, east, north):
    inner = padded[:, :, 1:-1, 1:-1]
    west_cell = padded[:, :, :-2, 1:-1]
    east_cell = padded[:, :, 2:, 1:-1]
    south_cell = padded[:, :, 1:-1, :-2]
    north_cell = padded[:, :, 1:-1, 2:]
    return (inner - jnp.maximum(east, 0.0) * (inner - west_cell)
            - jnp.maximum(-east, 0.0) * (inner - east_cell)
            - jnp.maximum(north, 0.0) * (inner - south_cell)
            - jnp.maximum(-north, 0.0) * (inner - north_cell))


def reference(spectrum, courant, decay, land, ice_rows, ice_route, wave_source):
    capacity = CX * CY // N_TILE + CX * CY // N_TILE // 2
    xpos = jnp.arange(NX).astype(jnp.int32)[:, None]
    ypos = jnp.arange(NY).astype(jnp.int32)[None, :]
    group = ypos // CY
    owner = xpos // CX
    cell_key = ((group * N_TILE + owner) * N_TILE + wave_source[0]) * capacity + wave_source[1]
    flat_cell = xpos * NY + ypos
    table = jnp.zeros((N_GRP * N_TILE * N_TILE * capacity,), jnp.int32)
    table = table.at[cell_key.reshape(-1)].set(flat_cell.reshape(-1).astype(jnp.int32))
    rowpos = jnp.arange(ROWS).astype(jnp.int32)
    block = rowpos // (CX * CY)
    row_group = block // N_TILE
    sender = block % N_TILE
    row_key = ((row_group * N_TILE + ice_route[0]) * N_TILE + sender) * capacity + ice_route[1]
    target = table[row_key]
    field = jnp.zeros((3, NX * NY), jnp.float32).at[:, target].set(ice_rows).reshape(3, NX, NY)
    concentration, thickness, floe = field[0], field[1], field[2]
    freq = jnp.arange(K).astype(jnp.float32)
    wavelen = jnp.exp(-0.2 * freq)[:, None, None]
    rate = decay[:, None, None] * concentration[None] * (thickness[None] + wavelen / (wavelen + floe[None]))
    factor = land.astype(jnp.float32)[None] * jnp.exp(-rate)
    angle = 2.0 * jnp.pi * (jnp.arange(TH).astype(jnp.float32) + 0.5) / TH
    cosine = jnp.cos(angle)
    sine = jnp.sin(angle)
    east = (cosine[:, None] * courant[None, :])[:, :, None, None]
    north = (sine[:, None] * courant[None, :])[:, :, None, None]
    energy = spectrum.reshape(TH, K, N_GRP, N_TILE, CX, CY).transpose(0, 1, 3, 4, 2, 5).reshape(TH, K, NX, NY)
    for substep in range(2):
        padded = jnp.pad(energy, ((0, 0), (0, 0), (1, 1), (1, 1)))
        energy = factor[None] * advect(padded, east, north)
    zonal = jnp.einsum("tkxy,t->kxy", energy, cosine, precision=lax.Precision.HIGHEST)
    meridional = jnp.einsum("tkxy,t->kxy", energy, sine, precision=lax.Precision.HIGHEST)
    raw_weight = jnp.exp(0.1 * freq)
    weights = 3.0 * raw_weight / jnp.sum(raw_weight)
    stokes_x = jnp.einsum("kxy,k->xy", zonal, weights, precision=lax.Precision.HIGHEST)
    stokes_y = jnp.einsum("kxy,k->xy", meridional, weights, precision=lax.Precision.HIGHEST)
    stress_x = jnp.sum(rate * zonal, 0) * (4.0 / K)
    stress_y = jnp.sum(rate * meridional, 0) * (4.0 / K)
    values = jnp.stack([stokes_x, stokes_y, stress_x, stress_y]).reshape(4, NX * NY)
    coupling = values[:, target]
    flat_out = energy.reshape(TH, K, N_TILE, CX, N_GRP, CY).transpose(0, 1, 4, 2, 3, 5).reshape(TH, K, CELLS)
    return flat_out, coupling
```

```python
import functools
import math

import jax
import jax.numpy as jnp
from jax import lax
from jax.experimental import pallas as pl
from jax.experimental.pallas import tpu as pltpu
from jax.sharding import PartitionSpec as P

MESH = pl.DeviceIdType.MESH
F32 = jnp.float32
DIRS, FREQS, LANES, CELLS = 36, 36, 128, 256
SIDE = 16
NINE = 9
QUADS = ((0, 0), (1, 0), (1, 1), (0, 1))
X_START = (9, 0, 9, 0)


def dot(a, b, dims):
    return lax.dot_general(a, b, (dims, ((), ())), precision=lax.Precision.HIGHEST, preferred_element_type=F32)


def roll(value, shift):
    return pltpu.roll(value, shift, 1)


def kernel(
    n_grp, n_tile,
    spec_hbm, cour_hbm, decay_hbm, land_hbm, ice_hbm, route_hbm, source_hbm,
    out_hbm, coup_ref,
    e0, u0, cour_in, decay_in, land_in, ice_in, route_in, source_in,
    cos_tab, sin_tab, cour_ref, decay_ref, factor_ref, rate_ref, zonal_ref, merid_ref,
    xs, xr, xinfo_s, xinfo_r, ys, yr, cs, cr, yf_s, yf_r,
    rows_s, rows_r, back_s, back_r,
    in_sem, spec_sem, out_sem, send_sem, x_sem, xinfo_sem, y_sem, c_sem, yf_sem, rows_sem, back_sem,
):
    g = lax.axis_index("grp")
    t = lax.axis_index("tile")
    half = n_tile // 2

    def partner(n):
        step = (n + 1) // 2
        return lax.rem(t + half + jnp.where(n % 2 == 1, step, -step), n_tile)

    t_next, t_prev = lax.rem(t + 1, n_tile), lax.rem(t + n_tile - 1, n_tile)
    g_next, g_prev = lax.rem(g + 1, n_grp), lax.rem(g + n_grp - 1, n_grp)
    x_to = ((g, t_next), (g, t_prev))
    y_to = ((g_next, t), (g_prev, t))
    c_to = tuple((y_to[y][0], x_to[x][1]) for x, y in QUADS)

    barrier = pltpu.get_barrier_semaphore()

    def greet(n, carry):
        pl.semaphore_signal(barrier, inc=1, device_id=(g, partner(n)), device_id_type=MESH)
        return carry

    lax.fori_loop(0, n_tile - 1, greet, 0)
    for device in y_to + c_to:
        pl.semaphore_signal(barrier, inc=1, device_id=device, device_id_type=MESH)

    small = [
        pltpu.make_async_copy(src, dst, in_sem.at[i])
        for i, (src, dst) in enumerate((
            (ice_hbm, ice_in), (route_hbm, route_in), (cour_hbm, cour_in),
            (decay_hbm, decay_in), (land_hbm, land_in), (source_hbm, source_in),
        ))
    ]
    for copy in small:
        copy.start()
    big = [
        pltpu.make_async_copy(spec_hbm.at[pl.ds(NINE * q, NINE)], e0.at[pl.ds(NINE * q, NINE)], spec_sem.at[q])
        for q in range(4)
    ]
    for copy in big:
        copy.start()

    edge_x = (jnp.where(t > 0, 1.0, 0.0).astype(F32), jnp.where(t < n_tile - 1, 1.0, 0.0).astype(F32))
    edge_y = (jnp.where(g > 0, 1.0, 0.0).astype(F32), jnp.where(g < n_grp - 1, 1.0, 0.0).astype(F32))

    for j in range(DIRS):
        angle = 2.0 * math.pi * (j + 0.5) / DIRS
        cos_tab[j] = jnp.full((1, LANES), abs(math.cos(angle)), F32)
        sin_tab[j] = jnp.full((1, LANES), abs(math.sin(angle)), F32)
    for ref in (xs, ys, cs):
        ref[...] = jnp.zeros(ref.shape, F32)

    lane = lax.broadcasted_iota(jnp.int32, (FREQS, LANES), 1)
    slot16 = lane // SIDE
    pos16 = lane % SIDE
    freq = lax.broadcasted_iota(jnp.int32, (FREQS, LANES), 0).astype(F32)
    wavelen = jnp.exp(-0.2 * freq)

    for copy in small:
        copy.wait()

    eye = lax.broadcasted_iota(jnp.int32, (FREQS, FREQS), 0) == lax.broadcasted_iota(jnp.int32, (FREQS, FREQS), 1)

    def column(row):
        picked = jnp.where(eye, jnp.broadcast_to(row, (FREQS, FREQS)), 0.0)
        return jnp.broadcast_to(jnp.sum(picked, axis=1, keepdims=True), (FREQS, LANES))

    cour_ref[...] = column(cour_in[...])
    decay_ref[...] = column(decay_in[...])

    slot8 = lax.broadcasted_iota(jnp.int32, (8, CELLS), 0)
    tiles = lax.broadcasted_iota(jnp.int32, (n_tile, CELLS), 0)
    dest, dest_slot = route_in[0:1], route_in[1:2]
    to_dest = jnp.where(tiles == dest, 1.0, 0.0).astype(F32)
    lanes_of = jnp.concatenate(
        [jnp.where(slot8 == dest_slot, ice_in[c:c + 1], 0.0) for c in range(3)]
        + [jnp.zeros((LANES - 24, CELLS), F32)], axis=0)
    table = dot(to_dest, lanes_of, ((1,), (1,)))
    table = (
        pltpu.roll(table, 1, 0) + roll(table, 32) + roll(pltpu.roll(table, n_tile - 1, 0), 64)
    )
    rows_s[...] = table.reshape(n_tile, 1, LANES)

    cell_y = lax.broadcasted_iota(jnp.int32, (SIDE, CELLS), 1)
    row16 = lax.broadcasted_iota(jnp.int32, (SIDE, CELLS), 0)
    spread = jnp.where(cell_y % SIDE == row16, 1.0, 0.0).astype(F32)

    def flat(grid):
        wide = dot(grid.astype(F32), spread, ((1,), (0,)))
        return jnp.sum(jnp.where(cell_y // SIDE == row16, wide, 0.0), axis=0, keepdims=True)

    source, slot, land = flat(source_in[0]), flat(source_in[1]), flat(land_in[...])
    own = jnp.concatenate([source, slot, land, jnp.zeros((5, CELLS), F32)], axis=0)
    lane8 = lax.broadcasted_iota(jnp.int32, (8, LANES), 1)
    for side in range(2):
        if side == 0:
            edge = jnp.where(lane8 < SIDE, roll(own[:, LANES:], SIDE), 0.0)
        else:
            edge = jnp.where(lane8 < SIDE, own[:, :LANES], 0.0)
        for shift in (16, 32, 64):
            edge = edge + roll(edge, shift)
        xinfo_s[side] = edge

    def sides(q):
        return QUADS[q]

    def packed(q, j):
        i = X_START[q] + j
        group = i // 8
        return group, i - 8 * group

    def first(q):
        sx, sy = sides(q)

        def step(j, carry):
            d = NINE * q + j
            low, high = e0[d, :, 0:LANES], e0[d, :, LANES:CELLS]
            cour = cour_ref[...]
            ax, ay = cour * cos_tab[d], cour * sin_tab[d]
            keep = 1.0 - ax - ay
            if sx == 0:
                rl, rh = roll(low, SIDE), roll(high, SIDE)
                xl, xh = jnp.where(lane < SIDE, 0.0, rl), jnp.where(lane < SIDE, rl, rh)
            else:
                rl, rh = roll(low, LANES - SIDE), roll(high, LANES - SIDE)
                xl, xh = jnp.where(lane >= LANES - SIDE, rh, rl), jnp.where(lane >= LANES - SIDE, 0.0, rh)
            if sy == 0:
                yl = jnp.where(pos16 == 0, 0.0, roll(low, 1))
                yh = jnp.where(pos16 == 0, 0.0, roll(high, 1))
            else:
                yl = jnp.where(pos16 == SIDE - 1, 0.0, roll(low, LANES - 1))
                yh = jnp.where(pos16 == SIDE - 1, 0.0, roll(high, LANES - 1))
            ul = keep * low + ax * xl + ay * yl
            uh = keep * high + ax * xh + ay * yh
            u0[d, :, 0:LANES] = ul
            u0[d, :, LANES:CELLS] = uh
            group, place = packed(q, j)
            shift = lax.rem(16 * place + (16 if sx == 0 else 0), LANES)
            here = slot16 == place
            for kind, pair in enumerate(((low, high), (ul, uh))):
                edge = pair[1] if sx == 0 else pair[0]
                at = 3 * kind + group
                xs[sx, at] = jnp.where(here, roll(edge, shift), xs[sx, at])
            shift = lax.rem(j + (113 if sy == 0 else 0), LANES)
            here = pos16 == j
            arr = q % 2
            for kind, pair in enumerate(((low, high), (ul, uh))):
                at = 2 * kind + arr
                for part in range(2):
                    cut = slice(LANES * part, LANES * (part + 1))
                    ys[sy, at, :, cut] = jnp.where(here, roll(pair[part], shift), ys[sy, at, :, cut])
            corner = high if sx == 0 else low
            lies = (LANES - SIDE if sx == 0 else 0) + (SIDE - 1 if sy == 0 else 0)
            goes = 16 * place + (0 if sy == 0 else SIDE - 1)
            at = group - X_START[q] // 8
            cs[q, at] = jnp.where(lane == goes, roll(corner, lax.rem(goes - lies + LANES, LANES)), cs[q, at])
            goes = j + (0 if sx == 0 else LANES - SIDE)
            cs[q, 2] = jnp.where(lane == goes, roll(corner, lax.rem(goes - lies + LANES, LANES)), cs[q, 2])
            return carry

        lax.fori_loop(0, NINE, step, 0)

    for q in range(4):
        big[q].wait()
        first(q)

    pl.semaphore_wait(barrier, n_tile - 1 + 6)

    def send_row(src, dst, sem):
        def step(n, carry):
            d = partner(n)
            pltpu.make_async_remote_copy(
                src_ref=src.at[d], dst_ref=dst.at[t], send_sem=send_sem.at[0], recv_sem=sem.at[0],
                device_id=(g, d), device_id_type=MESH).start()
            return carry

        lax.fori_loop(0, n_tile - 1, step, 0)
        dst[pl.ds(t, 1)] = src[pl.ds(t, 1)]

    def rows_wait(ref, sem):
        view = ref.at[pl.ds(0, n_tile - 1)]
        pltpu.make_async_copy(view, view, sem.at[0]).wait()

    send_row(rows_s, rows_r, rows_sem)

    def remote(src, dst, sent, arrived, device):
        return pltpu.make_async_remote_copy(
            src_ref=src, dst_ref=dst, send_sem=sent, recv_sem=arrived, device_id=device, device_id_type=MESH)

    x_copy = [remote(xs.at[s], xr.at[s], send_sem.at[1 + s], x_sem.at[s], x_to[s]) for s in range(2)]
    i_copy = [remote(xinfo_s.at[s], xinfo_r.at[s], send_sem.at[3 + s], xinfo_sem.at[s], x_to[s]) for s in range(2)]
    y_copy = [remote(ys.at[s], yr.at[s], send_sem.at[5 + s], y_sem.at[s], y_to[s]) for s in range(2)]
    c_copy = [remote(cs.at[q], cr.at[q], send_sem.at[7 + q], c_sem.at[q], c_to[q]) for q in range(4)]
    for copy in i_copy + x_copy + y_copy + c_copy:
        copy.start()

    for copy in i_copy:
        copy.wait_recv()
    sources = jnp.concatenate([source, xinfo_r[0, 0:1], xinfo_r[1, 0:1]], axis=1)
    wide = lax.broadcasted_iota(jnp.int32, (n_tile, CELLS + 2 * LANES), 0).astype(F32)
    from_source = jnp.where(wide == sources, 1.0, 0.0).astype(F32)

    for copy in x_copy + y_copy + c_copy:
        copy.wait_recv()

    def halo_x(q, j, ref_value):
        sx, _ = sides(q)
        _, place = packed(q, j)
        shift = lax.rem((LANES if sx == 0 else 2 * LANES - SIDE) - 16 * place, LANES)
        return roll(ref_value, shift)

    def halo_y(q, j, value):
        _, sy = sides(q)
        return roll(value, lax.rem((LANES if sy == 0 else LANES + SIDE - 1) - j, LANES))

    def second(q):
        sx, sy = sides(q)

        def step(j, carry):
            d = NINE * q + j
            cour = cour_ref[...]
            ax, ay = cour * cos_tab[d] * edge_x[sx], cour * sin_tab[d] * edge_y[sy]
            group, _ = packed(q, j)
            hx = ax * halo_x(q, j, xr[sx, group])
            rim = pos16 == (0 if sy == 0 else SIDE - 1)
            hl = jnp.where(rim, ay * halo_y(q, j, yr[sy, q % 2, :, 0:LANES]), 0.0)
            hh = jnp.where(rim, ay * halo_y(q, j, yr[sy, q % 2, :, LANES:CELLS]), 0.0)
            if sx == 0:
                hl = hl + jnp.where(lane < SIDE, hx, 0.0)
            else:
                hh = hh + jnp.where(lane >= LANES - SIDE, hx, 0.0)
            u0[d, :, 0:LANES] = u0[d, :, 0:LANES] + hl
            u0[d, :, LANES:CELLS] = u0[d, :, LANES:CELLS] + hh
            return carry

        lax.fori_loop(0, NINE, step, 0)

    for q in range(4):
        second(q)

    turn = [10.0 * (j + 0.5) * math.pi / 180.0 for j in range(NINE)]
    for group in range(3):
        weight = jnp.zeros((FREQS, LANES), F32)
        for place in range(8):
            i = 8 * group + place
            if i < 18:
                value = math.cos(turn[i]) if i < NINE else math.sin(turn[i - NINE])
                weight = jnp.where(slot16 == place, value, weight)
        weight = weight * cour_ref[...]
        for q in range(4):
            sx, sy = sides(q)
            at = group - X_START[q] // 8
            if 0 <= at < 2:
                xr[sx, 3 + group] = xr[sx, 3 + group] + weight * (edge_y[sy] * cr[q, at])
    for arr in range(2):
        weight = jnp.zeros((FREQS, LANES), F32)
        for j in range(NINE):
            weight = jnp.where(pos16 == j, math.cos(turn[j]) if arr == 0 else math.sin(turn[j]), weight)
        weight = weight * cour_ref[...]
        for q in (arr, arr + 2):
            sx, sy = sides(q)
            cut = slice(0, LANES) if sx == 0 else slice(LANES, CELLS)
            yr[sy, 2 + arr, :, cut] = yr[sy, 2 + arr, :, cut] + weight * (edge_x[sx] * cr[q, 2])

    rows_wait(rows_r, rows_sem)
    arrived = rows_r[...].reshape(n_tile, LANES).T
    found = dot(arrived, from_source, ((1,), (0,)))

    def pick(section, cut, slots):
        width = slots.shape[1]
        mask = lax.broadcasted_iota(jnp.int32, (8, width), 0).astype(F32) == slots
        return [
            jnp.sum(jnp.where(mask, found[32 * section + 8 * c:32 * section + 8 * c + 8, cut], 0.0), axis=0, keepdims=True)
            for c in range(3)
        ]

    field = pick(1, slice(0, CELLS), slot)
    near = [
        pick(2 * s, slice(CELLS + LANES * s, CELLS + LANES * (s + 1)), xinfo_r[s, 1:2]) for s in range(2)
    ]

    fields = jnp.concatenate(field + [land, jnp.zeros((4, CELLS), F32)], axis=0)
    pos8 = lane8 % SIDE
    for s in range(2):
        for part in range(2):
            cut = slice(LANES * part, LANES * (part + 1))
            edge = jnp.where(pos8 == (SIDE - 1 if s == 0 else 0), fields[:, cut], 0.0)
            for shift in (1, 2, 4, 8):
                edge = edge + roll(edge, LANES - shift if s == 0 else shift)
            yf_s[s, :, cut] = edge
    f_copy = [remote(yf_s.at[s], yf_r.at[s], send_sem.at[11 + s], yf_sem.at[s], y_to[s]) for s in range(2)]
    for copy in f_copy:
        copy.start()

    def rate_of(values):
        conc, thick, floe = values
        return decay_ref[...] * conc * (thick + wavelen / (wavelen + floe))

    for part in range(2):
        cut = slice(LANES * part, LANES * (part + 1))
        rate = rate_of([v[:, cut] for v in field])
        rate_ref[:, cut] = rate
        factor_ref[:, cut] = land[:, cut] * jnp.exp(-rate)
    for s in range(2):
        rim = (xinfo_r[s, 2:3] * edge_x[s]) * jnp.exp(-rate_of(near[s]))
        for group in range(3):
            xr[s, 3 + group] = xr[s, 3 + group] * rim

    def scale(d, carry):
        u0[d] = u0[d] * factor_ref[...]
        return carry

    lax.fori_loop(0, DIRS, scale, 0)

    for copy in f_copy:
        copy.wait_recv()
    for s in range(2):
        for part in range(2):
            cut = slice(LANES * part, LANES * (part + 1))
            rim = (yf_r[s, 3:4, cut] * edge_y[s]) * jnp.exp(-rate_of([yf_r[s, c:c + 1, cut] for c in range(3)]))
            for arr in range(2):
                yr[s, 2 + arr, :, cut] = yr[s, 2 + arr, :, cut] * rim

    zonal_ref[...] = jnp.zeros((FREQS, CELLS), F32)
    merid_ref[...] = jnp.zeros((FREQS, CELLS), F32)

    def third(q):
        sx, sy = sides(q)

        def step(j, carry):
            d = NINE * q + j
            low, high = u0[d, :, 0:LANES], u0[d, :, LANES:CELLS]
            cour = cour_ref[...]
            cx, sn = cos_tab[d], sin_tab[d]
            ax, ay = cour * cx, cour * sn
            keep = 1.0 - ax - ay
            group, _ = packed(q, j)
            hx = halo_x(q, j, xr[sx, 3 + group])
            if sx == 0:
                rl, rh = roll(low, SIDE), roll(high, SIDE)
                xl, xh = jnp.where(lane < SIDE, hx, rl), jnp.where(lane < SIDE, rl, rh)
            else:
                rl, rh = roll(low, LANES - SIDE), roll(high, LANES - SIDE)
                xl, xh = jnp.where(lane >= LANES - SIDE, rh, rl), jnp.where(lane >= LANES - SIDE, hx, rh)
            shift, rim = (1, pos16 == 0) if sy == 0 else (LANES - 1, pos16 == SIDE - 1)
            hl = halo_y(q, j, yr[sy, 2 + q % 2, :, 0:LANES])
            hh = halo_y(q, j, yr[sy, 2 + q % 2, :, LANES:CELLS])
            yl = jnp.where(rim, hl, roll(low, shift))
            yh = jnp.where(rim, hh, roll(high, shift))
            nl = factor_ref[:, 0:LANES] * (keep * low + ax * xl + ay * yl)
            nh = factor_ref[:, LANES:CELLS] * (keep * high + ax * xh + ay * yh)
            e0[d, :, 0:LANES] = nl
            e0[d, :, LANES:CELLS] = nh
            sc = cx if sx == 0 else -cx
            ss = sn if sy == 0 else -sn
            zonal_ref[:, 0:LANES] += sc * nl
            zonal_ref[:, LANES:CELLS] += sc * nh
            merid_ref[:, 0:LANES] += ss * nl
            merid_ref[:, LANES:CELLS] += ss * nh
            return carry

        lax.fori_loop(0, NINE, step, 0)

    result = [
        pltpu.make_async_copy(e0.at[pl.ds(NINE * q, NINE)], out_hbm.at[pl.ds(NINE * q, NINE)], out_sem.at[q])
        for q in range(4)
    ]
    for q in range(4):
        third(q)
        result[q].start()

    raw = jnp.exp(0.1 * freq)
    weight = 3.0 * raw / jnp.sum(raw, axis=0, keepdims=True)
    values = []
    for scaled in (False, True):
        for ref in (zonal_ref, merid_ref):
            parts = []
            for part in range(2):
                cut = slice(LANES * part, LANES * (part + 1))
                total = jnp.sum((rate_ref[:, cut] if scaled else weight) * ref[:, cut], axis=0, keepdims=True)
                parts.append(total * (4.0 / FREQS) if scaled else total)
            values.append(jnp.concatenate(parts, axis=1))
    picked = slot8.astype(F32) == slot
    lanes_of = jnp.concatenate(
        [jnp.where(picked, v, 0.0) for v in values] + [jnp.zeros((LANES - 32, CELLS), F32)], axis=0)
    back_s[...] = dot(from_source[:, 0:CELLS], lanes_of, ((1,), (1,))).reshape(n_tile, 1, LANES)
    rows_wait(rows_s, send_sem)
    send_row(back_s, back_r, back_sem)

    rows_wait(back_r, back_sem)
    found = dot(back_r[...].reshape(n_tile, LANES).T, to_dest, ((1,), (0,)))
    for c in range(4):
        coup_ref[c:c + 1] = jnp.sum(
            jnp.where(slot8 == dest_slot, found[8 * c:8 * c + 8], 0.0), axis=0, keepdims=True)

    rows_wait(back_s, send_sem)
    for copy in x_copy + i_copy + y_copy + c_copy + f_copy:
        copy.wait_send()
    for copy in result:
        copy.wait()


def solution(mesh):
    n_grp, n_tile = mesh.shape["grp"], mesh.shape["tile"]

    def body(spectrum, courant, decay, land, ice_rows, ice_route, wave_source):
        vmem = pltpu.VMEM
        dma = pltpu.SemaphoreType.DMA
        scratch = [
            vmem((DIRS, FREQS, CELLS), F32), vmem((DIRS, FREQS, CELLS), F32),
            vmem((1, FREQS), F32), vmem((1, FREQS), F32), vmem((SIDE, SIDE), jnp.int32),
            vmem((3, CELLS), F32), vmem((2, CELLS), jnp.int32), vmem((2, SIDE, SIDE), jnp.int32),
            vmem((DIRS, 1, LANES), F32), vmem((DIRS, 1, LANES), F32),
            vmem((FREQS, LANES), F32), vmem((FREQS, LANES), F32),
            vmem((FREQS, CELLS), F32), vmem((FREQS, CELLS), F32),
            vmem((FREQS, CELLS), F32), vmem((FREQS, CELLS), F32),
            vmem((2, 6, FREQS, LANES), F32), vmem((2, 6, FREQS, LANES), F32),
            vmem((2, 8, LANES), F32), vmem((2, 8, LANES), F32),
            vmem((2, 4, FREQS, CELLS), F32), vmem((2, 4, FREQS, CELLS), F32),
            vmem((4, 3, FREQS, LANES), F32), vmem((4, 3, FREQS, LANES), F32),
            vmem((2, 8, CELLS), F32), vmem((2, 8, CELLS), F32),
            vmem((n_tile, 1, LANES), F32), vmem((n_tile, 1, LANES), F32),
            vmem((n_tile, 1, LANES), F32), vmem((n_tile, 1, LANES), F32),
            dma((6,)), dma((4,)), dma((4,)), dma((13,)), dma((2,)), dma((2,)), dma((2,)), dma((4,)), dma((2,)),
            dma((1,)), dma((1,)),
        ]
        return pl.pallas_call(
            functools.partial(kernel, n_grp, n_tile),
            out_shape=(
                jax.ShapeDtypeStruct((DIRS, FREQS, CELLS), F32),
                jax.ShapeDtypeStruct((4, CELLS), F32),
            ),
            in_specs=[pl.BlockSpec(memory_space=pl.ANY)] * 7,
            out_specs=(pl.BlockSpec(memory_space=pl.ANY), pl.BlockSpec(memory_space=pltpu.VMEM)),
            scratch_shapes=scratch,
            name="coupling_step",
            compiler_params=pltpu.CompilerParams(
                collective_id=0, has_side_effects=True, vmem_limit_bytes=60 * 1024 * 1024),
        )(spectrum, courant.reshape(1, FREQS), decay.reshape(1, FREQS), land, ice_rows, ice_route, wave_source)

    in_specs = (
        P(None, None, ("grp", "tile")),
        P(),
        P(),
        P("tile", "grp"),
        P(None, ("grp", "tile")),
        P(None, ("grp", "tile")),
        P(None, "tile", "grp"),
    )
    out_specs = (P(None, None, ("grp", "tile")), P(None, ("grp", "tile")))
    return jax.shard_map(body, mesh=mesh, in_specs=in_specs, out_specs=out_specs, check_vma=False)
```

```python
import functools
import math

import jax
import jax.numpy as jnp
from jax import lax
from jax.experimental import pallas as pl
from jax.experimental.pallas import tpu as pltpu
from jax.sharding import PartitionSpec as P

MESH = pl.DeviceIdType.MESH
F32 = jnp.float32
DIRS, FREQS, LANES, CELLS = 36, 36, 128, 256
SIDE = 16
NINE = 9
QUADS = ((0, 0), (1, 0), (1, 1), (0, 1))
X_START = (9, 0, 9, 0)
TURN = [(j + 0.5) * math.pi / 18.0 for j in range(NINE)]
HALVES = (slice(0, LANES), slice(LANES, CELLS))


def size(q, j):
    pair = math.cos(TURN[j]), math.sin(TURN[j])
    return pair if q % 2 == 0 else pair[::-1]


def place_of(q, j):
    return divmod(X_START[q] + j, 8)


def dot(a, b, dims):
    return lax.dot_general(a, b, (dims, ((), ())), precision=lax.Precision.HIGHEST, preferred_element_type=F32)


def roll(value, shift):
    shift %= value.shape[1]
    return pltpu.roll(value, shift, 1) if shift else value


def kernel(
    n_grp, n_tile,
    spec_hbm, cour_hbm, decay_hbm, land_hbm, ice_hbm, route_hbm, source_hbm,
    e0, back_r,
    u0, cour_in, decay_in, land_in, ice_in, route_in, source_in,
    weights, cour_ref, decay_ref, factor_ref, rate_ref, zonal_ref, merid_ref,
    xs, xr, xinfo_s, xinfo_r, ys, yr, cs, cr, yf_s, yf_r,
    rows_s, rows_r, back_s,
    in_sem, spec_sem, send_sem, x_sem, xinfo_sem, y_sem, c_sem, yf_sem, rows_sem, back_sem,
):
    g = lax.axis_index("grp")
    t = lax.axis_index("tile")
    half = n_tile // 2

    def partner(n):
        step = (n + 1) // 2
        return lax.rem(t + half + jnp.where(n % 2 == 1, step, -step), n_tile)

    t_next, t_prev = lax.rem(t + 1, n_tile), lax.rem(t + n_tile - 1, n_tile)
    g_next, g_prev = lax.rem(g + 1, n_grp), lax.rem(g + n_grp - 1, n_grp)
    x_to = ((g, t_next), (g, t_prev))
    y_to = ((g_next, t), (g_prev, t))
    c_to = tuple((y_to[y][0], x_to[x][1]) for x, y in QUADS)

    barrier = pltpu.get_barrier_semaphore()

    def greet(n, carry):
        pl.semaphore_signal(barrier, inc=1, device_id=(g, partner(n)), device_id_type=MESH)
        return carry

    lax.fori_loop(0, n_tile - 1, greet, 0)
    for device in y_to + c_to:
        pl.semaphore_signal(barrier, inc=1, device_id=device, device_id_type=MESH)

    small = [
        pltpu.make_async_copy(src, dst, in_sem.at[i])
        for i, (src, dst) in enumerate((
            (ice_hbm, ice_in), (route_hbm, route_in), (cour_hbm, cour_in),
            (decay_hbm, decay_in), (land_hbm, land_in), (source_hbm, source_in),
        ))
    ]
    for copy in small:
        copy.start()
    big = [
        pltpu.make_async_copy(spec_hbm.at[pl.ds(NINE * q, NINE)], e0.at[pl.ds(NINE * q, NINE)], spec_sem.at[q])
        for q in range(4)
    ]
    for copy in big:
        copy.start()

    edge_x = (jnp.where(t > 0, 1.0, 0.0).astype(F32), jnp.where(t < n_tile - 1, 1.0, 0.0).astype(F32))
    edge_y = (jnp.where(g > 0, 1.0, 0.0).astype(F32), jnp.where(g < n_grp - 1, 1.0, 0.0).astype(F32))

    def masks(height):
        lane = lax.broadcasted_iota(jnp.int32, (height, LANES), 1)
        slot16, pos16 = lane // SIDE, lane % SIDE
        return lane, slot16, pos16, (lane < SIDE, lane >= LANES - SIDE), (pos16 == 0, pos16 == SIDE - 1)

    lane, slot16, pos16, _, _ = masks(8)

    for group in range(3):
        for kind in range(2):
            weight = jnp.zeros((8, LANES), F32)
            for q in (0, 1):
                for j in range(NINE):
                    if place_of(q, j)[0] == group:
                        weight = jnp.where(slot16 == place_of(q, j)[1], size(q, j)[kind], weight)
            weights[3 * kind + group] = weight
    for arr in range(2):
        for kind in range(2):
            weight = jnp.zeros((8, LANES), F32)
            for j in range(NINE):
                weight = jnp.where(pos16 == j, size(arr, j)[kind], weight)
            weights[6 + 2 * kind + arr] = weight

    for copy in small:
        copy.wait()

    eye = lax.broadcasted_iota(jnp.int32, (FREQS, FREQS), 0) == lax.broadcasted_iota(jnp.int32, (FREQS, FREQS), 1)

    def column(row):
        picked = jnp.where(eye, jnp.broadcast_to(row, (FREQS, FREQS)), 0.0)
        return jnp.broadcast_to(jnp.sum(picked, axis=1, keepdims=True), (FREQS, LANES))

    cour_ref[...] = column(cour_in[...])
    decay_ref[...] = column(decay_in[...])

    slot8 = lax.broadcasted_iota(jnp.int32, (8, CELLS), 0)
    tiles = lax.broadcasted_iota(jnp.int32, (n_tile, CELLS), 0)
    dest, dest_slot = route_in[0:1], route_in[1:2]
    to_dest = jnp.where(tiles == dest, 1.0, 0.0).astype(F32)
    lanes_of = jnp.concatenate(
        [jnp.where(slot8 == dest_slot, ice_in[c:c + 1], 0.0) for c in range(3)]
        + [jnp.zeros((LANES - 24, CELLS), F32)], axis=0)
    table = dot(to_dest, lanes_of, ((1,), (1,)))
    table = (
        pltpu.roll(table, 1, 0) + roll(table, 32) + roll(pltpu.roll(table, n_tile - 1, 0), 64)
    )
    rows_s[...] = table.reshape(n_tile, 1, LANES)

    cell_y = lax.broadcasted_iota(jnp.int32, (SIDE, CELLS), 1)
    row16 = lax.broadcasted_iota(jnp.int32, (SIDE, CELLS), 0)
    spread = jnp.where(cell_y % SIDE == row16, 1.0, 0.0).astype(F32)

    def flat(grid):
        wide = dot(grid.astype(F32), spread, ((1,), (0,)))
        return jnp.sum(jnp.where(cell_y // SIDE == row16, wide, 0.0), axis=0, keepdims=True)

    source, slot, land = flat(source_in[0]), flat(source_in[1]), flat(land_in[...])
    own = jnp.concatenate([source, slot, land, jnp.zeros((5, CELLS), F32)], axis=0)
    for side in range(2):
        if side == 0:
            edge = jnp.where(lane < SIDE, roll(own[:, LANES:], SIDE), 0.0)
        else:
            edge = jnp.where(lane < SIDE, own[:, :LANES], 0.0)
        for shift in (16, 32, 64):
            edge = edge + roll(edge, shift)
        xinfo_s[side] = edge

    def each_tile(body, carry=()):
        def step(n, carry):
            return tuple(a + b for a, b in zip(carry, body(pl.ds(pl.multiple_of(8 * n, 8), 8))))

        whole = FREQS // 8
        carry = lax.fori_loop(0, whole, step, carry)
        rest = body(pl.ds(8 * whole, FREQS - 8 * whole))
        return [jnp.sum(a, axis=0, keepdims=True) + jnp.sum(b, axis=0, keepdims=True) for a, b in zip(carry, rest)]

    def moved_x(first_x, sx, low, high, edge_low, edge_high):
        if sx == 0:
            rl, rh = roll(low, SIDE), roll(high, SIDE)
            return jnp.where(first_x[0], edge_low, rl), jnp.where(first_x[0], rl, rh)
        rl, rh = roll(low, -SIDE), roll(high, -SIDE)
        return jnp.where(first_x[1], rh, rl), jnp.where(first_x[1], edge_high, rh)

    def moved_y(first_y, sy, value):
        return jnp.where(first_y[sy], 0.0, roll(value, 1 if sy == 0 else -1))

    def halo_x(q, j, message):
        return roll(message, (0 if q in (0, 3) else LANES - SIDE) - SIDE * place_of(q, j)[1])

    def halo_y(q, j, message):
        return roll(message, (0 if q < 2 else SIDE - 1) - j)

    for copy in big:
        copy.wait()

    def first():
        _, slot16, pos16, first_x, first_y = masks(FREQS)
        cour = cour_ref[...]
        for q in (3, 0, 1, 2):
            sx, sy = QUADS[q]
            for j in range(NINE):
                d = NINE * q + j
                low, high = e0[d, :, HALVES[0]], e0[d, :, HALVES[1]]
                cx, sn = size(q, j)
                ax, ay = cour * cx, cour * sn
                keep = 1.0 - cour * (cx + sn)
                xl, xh = moved_x(first_x, sx, low, high, 0.0, 0.0)
                ul = keep * low + ax * xl + ay * moved_y(first_y, sy, low)
                uh = keep * high + ax * xh + ay * moved_y(first_y, sy, high)
                u0[d, :, HALVES[0]] = ul
                u0[d, :, HALVES[1]] = uh
                group, place = place_of(q, j)
                for kind, pair in enumerate(((low, high), (ul, uh))):
                    edge = roll(pair[1], SIDE * place + SIDE) if sx == 0 else roll(pair[0], SIDE * place)
                    at = 3 * kind + group
                    xs[sx, at] = jnp.where(slot16 == place, edge, xs[sx, at] if place else 0.0)
                    at = 2 * kind + q % 2
                    for half in range(2):
                        cut = HALVES[half]
                        edge = roll(pair[half], j - (SIDE - 1 if sy == 0 else 0))
                        ys[sy, at, :, cut] = jnp.where(pos16 == j, edge, ys[sy, at, :, cut] if j else 0.0)
        for q in range(4):
            sx, sy = QUADS[q]
            cs[q, 2] = roll(ys[sy, q % 2, :, HALVES[1 - sx]], SIDE if sx == 0 else -SIDE)
            for n in range(2):
                group = X_START[q] // 8 + n
                lies = [place_of(q, j)[1] for j in range(NINE) if place_of(q, j)[0] == group]
                mine = (slot16 >= lies[0]) & (slot16 <= lies[-1]) & first_y[sy]
                cs[q, n] = jnp.where(mine, roll(xs[sx, group], 1 - SIDE if sy == 0 else SIDE - 1), 0.0)

    first()

    pl.semaphore_wait(barrier, n_tile - 1 + 6)

    def send_row(src, dst, sem):
        def step(n, carry):
            d = partner(n)
            pltpu.make_async_remote_copy(
                src_ref=src.at[d], dst_ref=dst.at[t], send_sem=send_sem.at[0], recv_sem=sem.at[0],
                device_id=(g, d), device_id_type=MESH).start()
            return carry

        lax.fori_loop(0, n_tile - 1, step, 0)
        dst[pl.ds(t, 1)] = src[pl.ds(t, 1)]

    def rows_wait(ref, sem):
        view = ref.at[pl.ds(0, n_tile - 1)]
        pltpu.make_async_copy(view, view, sem.at[0]).wait()

    send_row(rows_s, rows_r, rows_sem)

    def remote(src, dst, sent, arrived, device):
        return pltpu.make_async_remote_copy(
            src_ref=src, dst_ref=dst, send_sem=sent, recv_sem=arrived, device_id=device, device_id_type=MESH)

    x_copy = [remote(xs.at[s], xr.at[s], send_sem.at[1 + s], x_sem.at[s], x_to[s]) for s in range(2)]
    i_copy = [remote(xinfo_s.at[s], xinfo_r.at[s], send_sem.at[3 + s], xinfo_sem.at[s], x_to[s]) for s in range(2)]
    y_copy = [remote(ys.at[s], yr.at[s], send_sem.at[5 + s], y_sem.at[s], y_to[s]) for s in range(2)]
    c_copy = [remote(cs.at[q], cr.at[q], send_sem.at[7 + q], c_sem.at[q], c_to[q]) for q in range(4)]
    for copy in i_copy + x_copy + y_copy + c_copy:
        copy.start()

    for copy in i_copy:
        copy.wait_recv()
    sources = jnp.concatenate([source, xinfo_r[0, 0:1], xinfo_r[1, 0:1]], axis=1)
    wide = lax.broadcasted_iota(jnp.int32, (n_tile, CELLS + 2 * LANES), 0).astype(F32)
    from_source = jnp.where(wide == sources, 1.0, 0.0).astype(F32)

    for copy in x_copy + y_copy + c_copy:
        copy.wait_recv()

    def second(rows):
        _, slot16, pos16, first_x, first_y = masks(rows.size)
        cour = cour_ref[rows]
        x_weight = [cour * weights[i, 0:rows.size] for i in range(6)]
        y_weight = [cour * weights[6 + i, 0:rows.size] for i in range(4)]
        for q in range(4):
            sx, sy = QUADS[q]
            x_edge = [x_weight[n] * (xr[sx, n, rows] * edge_x[sx]) for n in range(3)]
            y_edge = [y_weight[2 + q % 2] * (yr[sy, q % 2, rows, cut] * edge_y[sy]) for cut in HALVES]
            for j in range(NINE):
                d = NINE * q + j
                add = [jnp.where(first_y[sy], halo_y(q, j, y_edge[half]), 0.0) for half in range(2)]
                add[sx] = add[sx] + jnp.where(first_x[sx], halo_x(q, j, x_edge[place_of(q, j)[0]]), 0.0)
                for half in range(2):
                    u0[d, rows, HALVES[half]] = u0[d, rows, HALVES[half]] + add[half]
        for sx in range(2):
            corner = [jnp.zeros((rows.size, LANES), F32)] * 3
            for q in range(4):
                if QUADS[q][0] == sx:
                    for n in range(2):
                        group = X_START[q] // 8 + n
                        corner[group] = corner[group] + edge_y[QUADS[q][1]] * cr[q, n, rows]
            for n in range(3):
                whole = xr[sx, 3 + n, rows] + x_weight[3 + n] * corner[n]
                xr[sx, 3 + n, rows] = whole * (x_weight[n] * edge_x[sx])
        for q in range(4):
            sx, sy = QUADS[q]
            for half in range(2):
                whole = yr[sy, 2 + q % 2, rows, HALVES[half]]
                if half == sx:
                    corner = jnp.where(slot16 == (0 if sx == 0 else 7), cr[q, 2, rows], 0.0)
                    whole = whole + y_weight[q % 2] * (edge_x[sx] * corner)
                yr[sy, 2 + q % 2, rows, HALVES[half]] = whole * (y_weight[2 + q % 2] * edge_y[sy])
        return ()

    each_tile(second)

    rows_wait(rows_r, rows_sem)
    arrived = rows_r[...].reshape(n_tile, LANES).T
    found = dot(arrived, from_source, ((1,), (0,)))

    def pick(section, cut, slots):
        width = slots.shape[1]
        mask = lax.broadcasted_iota(jnp.int32, (8, width), 0).astype(F32) == slots
        return [
            jnp.sum(jnp.where(mask, found[32 * section + 8 * c:32 * section + 8 * c + 8, cut], 0.0), axis=0, keepdims=True)
            for c in range(3)
        ]

    field = pick(1, slice(0, CELLS), slot)
    near = [
        pick(2 * s, slice(CELLS + LANES * s, CELLS + LANES * (s + 1)), xinfo_r[s, 1:2]) for s in range(2)
    ]

    fields = jnp.concatenate(field + [land, jnp.zeros((4, CELLS), F32)], axis=0)
    for s in range(2):
        for part in range(2):
            cut = slice(LANES * part, LANES * (part + 1))
            edge = jnp.where(pos16 == (SIDE - 1 if s == 0 else 0), fields[:, cut], 0.0)
            for shift in (1, 2, 4, 8):
                edge = edge + roll(edge, -shift if s == 0 else shift)
            yf_s[s, :, cut] = edge
    f_copy = [remote(yf_s.at[s], yf_r.at[s], send_sem.at[11 + s], yf_sem.at[s], y_to[s]) for s in range(2)]
    for copy in f_copy:
        copy.start()

    def rate_of(rows, values):
        conc, thick, floe = values
        wavelen = jnp.exp(-0.2 * (lax.broadcasted_iota(jnp.int32, (rows.size, LANES), 0) + rows.start).astype(F32))
        return decay_ref[rows] * conc * (thick + wavelen / (wavelen + floe))

    near_land = [xinfo_r[s, 2:3] for s in range(2)]

    def third(rows):
        _, slot16, pos16, first_x, first_y = masks(rows.size)
        cour = cour_ref[rows]
        factor = []
        for half in range(2):
            cut = HALVES[half]
            rate = rate_of(rows, [v[:, cut] for v in field])
            rate_ref[rows, cut] = rate
            factor.append(land[:, cut] * jnp.exp(-rate))
            factor_ref[rows, cut] = factor[half]
        zonal, merid = [0.0, 0.0], [0.0, 0.0]
        for sx in range(2):
            rim = near_land[sx] * jnp.exp(-rate_of(rows, near[sx]))
            message = [xr[sx, 3 + n, rows] * rim for n in range(3)]
            for q in range(4):
                if QUADS[q][0] != sx:
                    continue
                sy = QUADS[q][1]
                for j in range(NINE):
                    d = NINE * q + j
                    low, high = u0[d, rows, HALVES[0]] * factor[0], u0[d, rows, HALVES[1]] * factor[1]
                    cx, sn = size(q, j)
                    ax, ay = cour * cx, cour * sn
                    keep = 1.0 - cour * (cx + sn)
                    hx = halo_x(q, j, message[place_of(q, j)[0]])
                    xl, xh = moved_x(first_x, sx, ax * low, ax * high, hx, hx)
                    new = (
                        factor[0] * (keep * low + xl + ay * moved_y(first_y, sy, low)),
                        factor[1] * (keep * high + xh + ay * moved_y(first_y, sy, high)),
                    )
                    for half in range(2):
                        e0[d, rows, HALVES[half]] = new[half]
                        zonal[half] = zonal[half] + (cx if sx == 0 else -cx) * new[half]
                        merid[half] = merid[half] + (sn if sy == 0 else -sn) * new[half]
        for half in range(2):
            zonal_ref[rows, HALVES[half]] = zonal[half]
            merid_ref[rows, HALVES[half]] = merid[half]
        return ()

    each_tile(third)

    for copy in f_copy:
        copy.wait_recv()

    raw_sum = sum(math.exp(0.1 * k) for k in range(FREQS))

    def fourth(rows):
        _, _, pos16, _, first_y = masks(rows.size)
        weight_of = [weights[6 + i, 0:rows.size] for i in range(4)]
        factor = [factor_ref[rows, cut] for cut in HALVES]
        zonal = [zonal_ref[rows, cut] for cut in HALVES]
        merid = [merid_ref[rows, cut] for cut in HALVES]
        for sy in range(2):
            inner = [jnp.where(first_y[sy], f, 0.0) for f in factor]
            message = [[], []]
            for half in range(2):
                cut = HALVES[half]
                rim = yf_r[sy, 3:4, cut] * jnp.exp(-rate_of(rows, [yf_r[sy, c:c + 1, cut] for c in range(3)]))
                message[half] = [yr[sy, 2 + arr, rows, cut] * rim for arr in range(2)]
            for q in (2 * sy, 2 * sy + 1):
                for j in range(NINE):
                    d = NINE * q + j
                    for half in range(2):
                        cut = HALVES[half]
                        e0[d, rows, cut] = e0[d, rows, cut] + inner[half] * halo_y(q, j, message[half][q % 2])
            for half in range(2):
                pair = message[half]
                sign = [1.0 if QUADS[2 * sy + arr][0] == 0 else -1.0 for arr in range(2)]
                along = sign[0] * weight_of[0] * pair[0] + sign[1] * weight_of[1] * pair[1]
                across = weight_of[2] * pair[0] + weight_of[3] * pair[1]
                if sy == 1:
                    across = -across
                for total, part in ((zonal, along), (merid, across)):
                    part = jnp.where(pos16 < NINE, part, 0.0)
                    for shift in (1, 2, 4, 8):
                        part = part + roll(part, -shift if sy == 0 else shift)
                    total[half] = total[half] + inner[half] * part
        k = lax.broadcasted_iota(jnp.int32, (rows.size, LANES), 0) + rows.start
        weight = jnp.exp(0.1 * k.astype(F32)) * (3.0 / raw_sum)
        out = []
        for scale in (None, rate_ref):
            for value in (zonal, merid):
                for half in range(2):
                    by = weight if scale is None else rate_ref[rows, HALVES[half]]
                    out.append(by * value[half])
        return out

    totals = each_tile(fourth, tuple(jnp.zeros((8, LANES), F32) for _ in range(8)))
    values = [jnp.concatenate(totals[2 * i:2 * i + 2], axis=1) * (1.0 if i < 2 else 4.0 / FREQS) for i in range(4)]
    picked = slot8.astype(F32) == slot
    lanes_of = jnp.concatenate(
        [jnp.where(picked, v, 0.0) for v in values] + [jnp.zeros((LANES - 32, CELLS), F32)], axis=0)
    back_s[...] = dot(from_source[:, 0:CELLS], lanes_of, ((1,), (1,))).reshape(n_tile, 1, LANES)
    rows_wait(rows_s, send_sem)
    send_row(back_s, back_r, back_sem)

    rows_wait(back_r, back_sem)
    rows_wait(back_s, send_sem)
    for copy in x_copy + i_copy + y_copy + c_copy + f_copy:
        copy.wait_send()


def finish(n_tile, e_ref, back_ref, route_hbm, out_hbm, coup_ref, route_in, in_sem, out_sem):
    copy = pltpu.make_async_copy(route_hbm, route_in, in_sem.at[0])
    copy.start()
    result = [
        pltpu.make_async_copy(
            e_ref.at[pl.ds(NINE * q, NINE)], out_hbm.at[pl.ds(NINE * q, NINE)], out_sem.at[q])
        for q in range(4)
    ]
    for part in result:
        part.start()
    copy.wait()
    tiles = lax.broadcasted_iota(jnp.int32, (n_tile, CELLS), 0)
    slot8 = lax.broadcasted_iota(jnp.int32, (8, CELLS), 0)
    to_dest = jnp.where(tiles == route_in[0:1], 1.0, 0.0).astype(F32)
    found = dot(back_ref[...].reshape(n_tile, LANES).T, to_dest, ((1,), (0,)))
    for c in range(4):
        coup_ref[c:c + 1] = jnp.sum(
            jnp.where(slot8 == route_in[1:2], found[8 * c:8 * c + 8], 0.0), axis=0, keepdims=True)
    for part in result:
        part.wait()


def solution(mesh):
    n_grp, n_tile = mesh.shape["grp"], mesh.shape["tile"]

    def body(spectrum, courant, decay, land, ice_rows, ice_route, wave_source):
        vmem = pltpu.VMEM
        dma = pltpu.SemaphoreType.DMA
        scratch = [
            vmem((DIRS, FREQS, CELLS), F32),
            vmem((1, FREQS), F32), vmem((1, FREQS), F32), vmem((SIDE, SIDE), jnp.int32),
            vmem((3, CELLS), F32), vmem((2, CELLS), jnp.int32), vmem((2, SIDE, SIDE), jnp.int32),
            vmem((10, 8, LANES), F32),
            vmem((FREQS, LANES), F32), vmem((FREQS, LANES), F32),
            vmem((FREQS, CELLS), F32), vmem((FREQS, CELLS), F32),
            vmem((FREQS, CELLS), F32), vmem((FREQS, CELLS), F32),
            vmem((2, 6, FREQS, LANES), F32), vmem((2, 6, FREQS, LANES), F32),
            vmem((2, 8, LANES), F32), vmem((2, 8, LANES), F32),
            vmem((2, 4, FREQS, CELLS), F32), vmem((2, 4, FREQS, CELLS), F32),
            vmem((4, 3, FREQS, LANES), F32), vmem((4, 3, FREQS, LANES), F32),
            vmem((2, 8, CELLS), F32), vmem((2, 8, CELLS), F32),
            vmem((n_tile, 1, LANES), F32), vmem((n_tile, 1, LANES), F32), vmem((n_tile, 1, LANES), F32),
            dma((6,)), dma((4,)), dma((13,)), dma((2,)), dma((2,)), dma((2,)), dma((4,)), dma((2,)),
            dma((1,)), dma((1,)),
        ]
        anywhere = pl.BlockSpec(memory_space=pl.ANY)
        held = pl.BlockSpec(memory_space=pltpu.VMEM)
        energy, back = pl.pallas_call(
            functools.partial(kernel, n_grp, n_tile),
            out_shape=(pltpu.VMEM((DIRS, FREQS, CELLS), F32), pltpu.VMEM((n_tile, 1, LANES), F32)),
            in_specs=[anywhere] * 7,
            out_specs=(held, held),
            scratch_shapes=scratch,
            name="coupling_step",
            compiler_params=pltpu.CompilerParams(
                collective_id=0, has_side_effects=True, vmem_limit_bytes=60 * 1024 * 1024),
        )(spectrum, courant.reshape(1, FREQS), decay.reshape(1, FREQS), land, ice_rows, ice_route, wave_source)
        return pl.pallas_call(
            functools.partial(finish, n_tile),
            out_shape=(
                jax.ShapeDtypeStruct((DIRS, FREQS, CELLS), F32),
                jax.ShapeDtypeStruct((4, CELLS), F32),
            ),
            in_specs=[held, held, anywhere],
            out_specs=(anywhere, held),
            scratch_shapes=[vmem((2, CELLS), jnp.int32), dma((1,)), dma((4,))],
            name="coupling_finish",
            compiler_params=pltpu.CompilerParams(vmem_limit_bytes=8 * 1024 * 1024),
        )(energy, back, ice_route)

    in_specs = (
        P(None, None, ("grp", "tile")),
        P(),
        P(),
        P("tile", "grp"),
        P(None, ("grp", "tile")),
        P(None, ("grp", "tile")),
        P(None, "tile", "grp"),
    )
    out_specs = (P(None, None, ("grp", "tile")), P(None, ("grp", "tile")))
    return jax.shard_map(body, mesh=mesh, in_specs=in_specs, out_specs=out_specs, check_vma=False)
```

```python
import functools
import math

import jax
import jax.numpy as jnp
from jax import lax
from jax.experimental import pallas as pl
from jax.experimental.pallas import tpu as pltpu
from jax.sharding import PartitionSpec as P

MESH = pl.DeviceIdType.MESH
F32 = jnp.float32
DIRS, FREQS, LANES, CELLS = 36, 36, 128, 256
SIDE = 16
NINE = 9
QUADS = ((0, 0), (1, 0), (1, 1), (0, 1))
X_START = (9, 0, 9, 0)
TURN = [(j + 0.5) * math.pi / 18.0 for j in range(NINE)]
HALVES = (slice(0, LANES), slice(LANES, CELLS))


def size(q, j):
    pair = math.cos(TURN[j]), math.sin(TURN[j])
    return pair if q % 2 == 0 else pair[::-1]


def place_of(q, j):
    return divmod(X_START[q] + j, 8)


def dot(a, b, dims):
    return lax.dot_general(a, b, (dims, ((), ())), precision=lax.Precision.HIGHEST, preferred_element_type=F32)


def split(value):
    high = value.astype(jnp.bfloat16)
    rest = value - high.astype(F32)
    middle = rest.astype(jnp.bfloat16)
    low = (rest - middle.astype(F32)).astype(jnp.bfloat16)
    return jnp.concatenate([high, middle, low], axis=0)


def gather(table, one_hot, rows):
    found = lax.dot_general(
        split(table.T[0:rows]), one_hot, (((1,), (0,)), ((), ())), preferred_element_type=F32)
    return found[0:rows] + found[rows:2 * rows] + found[2 * rows:]


def roll(value, shift):
    shift %= value.shape[1]
    return pltpu.roll(value, shift, 1) if shift else value


def kernel(
    n_grp, n_tile,
    spec_hbm, cour_hbm, decay_hbm, land_hbm, ice_hbm, route_hbm, source_hbm,
    e0, back_r,
    u0, cour_in, decay_in, land_in, ice_in, route_in, source_in,
    weights, cour_ref, decay_ref, factor_ref, rate_ref, zonal_ref, merid_ref,
    xs, xr, xinfo_s, xinfo_r, ys, yr, cs, cr, yf_s, yf_r,
    rows_s, rows_r, back_s,
    in_sem, spec_sem, send_sem, x_sem, xinfo_sem, y_sem, c_sem, yf_sem, rows_sem, back_sem,
):
    g = lax.axis_index("grp")
    t = lax.axis_index("tile")
    half = n_tile // 2

    def partner(n):
        step = (n + 1) // 2
        return lax.rem(t + half + jnp.where(n % 2 == 1, step, -step), n_tile)

    t_next, t_prev = lax.rem(t + 1, n_tile), lax.rem(t + n_tile - 1, n_tile)
    g_next, g_prev = lax.rem(g + 1, n_grp), lax.rem(g + n_grp - 1, n_grp)
    x_to = ((g, t_next), (g, t_prev))
    y_to = ((g_next, t), (g_prev, t))
    c_to = tuple((y_to[y][0], x_to[x][1]) for x, y in QUADS)

    barrier = pltpu.get_barrier_semaphore()

    def greet(n, carry):
        pl.semaphore_signal(barrier, inc=1, device_id=(g, partner(n)), device_id_type=MESH)
        return carry

    lax.fori_loop(0, n_tile - 1, greet, 0)
    for device in y_to + c_to:
        pl.semaphore_signal(barrier, inc=1, device_id=device, device_id_type=MESH)

    small = [
        pltpu.make_async_copy(src, dst, in_sem.at[i])
        for i, (src, dst) in enumerate((
            (ice_hbm, ice_in), (route_hbm, route_in), (cour_hbm, cour_in),
            (decay_hbm, decay_in), (land_hbm, land_in), (source_hbm, source_in),
        ))
    ]
    for copy in small:
        copy.start()
    big = [
        pltpu.make_async_copy(spec_hbm.at[pl.ds(NINE * q, NINE)], e0.at[pl.ds(NINE * q, NINE)], spec_sem.at[q])
        for q in range(4)
    ]
    for copy in big:
        copy.start()

    edge_x = (jnp.where(t > 0, 1.0, 0.0).astype(F32), jnp.where(t < n_tile - 1, 1.0, 0.0).astype(F32))
    edge_y = (jnp.where(g > 0, 1.0, 0.0).astype(F32), jnp.where(g < n_grp - 1, 1.0, 0.0).astype(F32))

    def masks(height):
        lane = lax.broadcasted_iota(jnp.int32, (height, LANES), 1)
        slot16, pos16 = lane // SIDE, lane % SIDE
        return lane, slot16, pos16, (lane < SIDE, lane >= LANES - SIDE), (pos16 == 0, pos16 == SIDE - 1)

    lane, slot16, pos16, _, _ = masks(8)

    for group in range(3):
        for kind in range(2):
            weight = jnp.zeros((8, LANES), F32)
            for q in (0, 1):
                for j in range(NINE):
                    if place_of(q, j)[0] == group:
                        weight = jnp.where(slot16 == place_of(q, j)[1], size(q, j)[kind], weight)
            weights[3 * kind + group] = weight
    for arr in range(2):
        for kind in range(2):
            weight = jnp.zeros((8, LANES), F32)
            for j in range(NINE):
                weight = jnp.where(pos16 == j, size(arr, j)[kind], weight)
            weights[6 + 2 * kind + arr] = weight

    for copy in small:
        copy.wait()

    eye = lax.broadcasted_iota(jnp.int32, (FREQS, FREQS), 0) == lax.broadcasted_iota(jnp.int32, (FREQS, FREQS), 1)

    def column(row):
        picked = jnp.where(eye, jnp.broadcast_to(row, (FREQS, FREQS)), 0.0)
        return jnp.broadcast_to(jnp.sum(picked, axis=1, keepdims=True), (FREQS, LANES))

    cour_ref[...] = column(cour_in[...])
    decay_ref[...] = column(decay_in[...])

    slot8 = lax.broadcasted_iota(jnp.int32, (8, CELLS), 0)
    tiles = lax.broadcasted_iota(jnp.int32, (n_tile, CELLS), 0)
    dest, dest_slot = route_in[0:1], route_in[1:2]
    to_dest = jnp.where(tiles == dest, 1.0, 0.0).astype(F32)
    lanes_of = jnp.concatenate(
        [jnp.where(slot8 == dest_slot, ice_in[c:c + 1], 0.0) for c in range(3)]
        + [jnp.zeros((LANES - 24, CELLS), F32)], axis=0)
    table = dot(to_dest, lanes_of, ((1,), (1,)))
    table = (
        pltpu.roll(table, 1, 0) + roll(table, 32) + roll(pltpu.roll(table, n_tile - 1, 0), 64)
    )
    rows_s[...] = table.reshape(n_tile, 1, LANES)

    cell_y = lax.broadcasted_iota(jnp.int32, (SIDE, CELLS), 1)
    row16 = lax.broadcasted_iota(jnp.int32, (SIDE, CELLS), 0)
    spread = jnp.where(cell_y % SIDE == row16, 1.0, 0.0).astype(F32)

    def flat(grid):
        wide = dot(grid.astype(F32), spread, ((1,), (0,)))
        return jnp.sum(jnp.where(cell_y // SIDE == row16, wide, 0.0), axis=0, keepdims=True)

    source, slot, land = flat(source_in[0]), flat(source_in[1]), flat(land_in[...])
    own = jnp.concatenate([source, slot, land, jnp.zeros((5, CELLS), F32)], axis=0)
    for side in range(2):
        if side == 0:
            edge = jnp.where(lane < SIDE, roll(own[:, LANES:], SIDE), 0.0)
        else:
            edge = jnp.where(lane < SIDE, own[:, :LANES], 0.0)
        for shift in (16, 32, 64):
            edge = edge + roll(edge, shift)
        xinfo_s[side] = edge

    def each_tile(body, carry=()):
        def step(n, carry):
            return tuple(a + b for a, b in zip(carry, body(pl.ds(pl.multiple_of(8 * n, 8), 8))))

        whole = FREQS // 8
        carry = lax.fori_loop(0, whole, step, carry)
        rest = body(pl.ds(8 * whole, FREQS - 8 * whole))
        return [jnp.sum(a, axis=0, keepdims=True) + jnp.sum(b, axis=0, keepdims=True) for a, b in zip(carry, rest)]

    def moved_x(first_x, sx, low, high, edge_low, edge_high):
        if sx == 0:
            rl, rh = roll(low, SIDE), roll(high, SIDE)
            return jnp.where(first_x[0], edge_low, rl), jnp.where(first_x[0], rl, rh)
        rl, rh = roll(low, -SIDE), roll(high, -SIDE)
        return jnp.where(first_x[1], rh, rl), jnp.where(first_x[1], edge_high, rh)

    def moved_y(first_y, sy, value):
        return jnp.where(first_y[sy], 0.0, roll(value, 1 if sy == 0 else -1))

    def halo_x(q, j, message):
        return roll(message, (0 if q in (0, 3) else LANES - SIDE) - SIDE * place_of(q, j)[1])

    def halo_y(q, j, message):
        return roll(message, (0 if q < 2 else SIDE - 1) - j)

    for copy in big:
        copy.wait()

    def first():
        _, slot16, pos16, first_x, first_y = masks(FREQS)
        cour = cour_ref[...]
        for q in (3, 0, 1, 2):
            sx, sy = QUADS[q]
            for j in range(NINE):
                d = NINE * q + j
                low, high = e0[d, :, HALVES[0]], e0[d, :, HALVES[1]]
                cx, sn = size(q, j)
                ax, ay = cour * cx, cour * sn
                keep = 1.0 - cour * (cx + sn)
                xl, xh = moved_x(first_x, sx, low, high, 0.0, 0.0)
                ul = keep * low + ax * xl + ay * moved_y(first_y, sy, low)
                uh = keep * high + ax * xh + ay * moved_y(first_y, sy, high)
                u0[d, :, HALVES[0]] = ul
                u0[d, :, HALVES[1]] = uh
                group, place = place_of(q, j)
                for kind, pair in enumerate(((low, high), (ul, uh))):
                    edge = roll(pair[1], SIDE * place + SIDE) if sx == 0 else roll(pair[0], SIDE * place)
                    at = 3 * kind + group
                    xs[sx, at] = jnp.where(slot16 == place, edge, xs[sx, at] if place else 0.0)
                    at = 2 * kind + q % 2
                    for half in range(2):
                        cut = HALVES[half]
                        edge = roll(pair[half], j - (SIDE - 1 if sy == 0 else 0))
                        ys[sy, at, :, cut] = jnp.where(pos16 == j, edge, ys[sy, at, :, cut] if j else 0.0)
        for q in range(4):
            sx, sy = QUADS[q]
            cs[q, 2] = roll(ys[sy, q % 2, :, HALVES[1 - sx]], SIDE if sx == 0 else -SIDE)
            for n in range(2):
                group = X_START[q] // 8 + n
                lies = [place_of(q, j)[1] for j in range(NINE) if place_of(q, j)[0] == group]
                mine = (slot16 >= lies[0]) & (slot16 <= lies[-1]) & first_y[sy]
                cs[q, n] = jnp.where(mine, roll(xs[sx, group], 1 - SIDE if sy == 0 else SIDE - 1), 0.0)

    first()

    pl.semaphore_wait(barrier, n_tile - 1 + 6)

    def send_row(src, dst, sem):
        def step(n, carry):
            d = partner(n)
            pltpu.make_async_remote_copy(
                src_ref=src.at[d], dst_ref=dst.at[t], send_sem=send_sem.at[0], recv_sem=sem.at[0],
                device_id=(g, d), device_id_type=MESH).start()
            return carry

        lax.fori_loop(0, n_tile - 1, step, 0)
        dst[pl.ds(t, 1)] = src[pl.ds(t, 1)]

    def rows_wait(ref, sem):
        view = ref.at[pl.ds(0, n_tile - 1)]
        pltpu.make_async_copy(view, view, sem.at[0]).wait()

    send_row(rows_s, rows_r, rows_sem)

    def remote(src, dst, sent, arrived, device):
        return pltpu.make_async_remote_copy(
            src_ref=src, dst_ref=dst, send_sem=sent, recv_sem=arrived, device_id=device, device_id_type=MESH)

    x_copy = [remote(xs.at[s], xr.at[s], send_sem.at[1 + s], x_sem.at[s], x_to[s]) for s in range(2)]
    i_copy = [remote(xinfo_s.at[s], xinfo_r.at[s], send_sem.at[3 + s], xinfo_sem.at[s], x_to[s]) for s in range(2)]
    y_copy = [remote(ys.at[s], yr.at[s], send_sem.at[5 + s], y_sem.at[s], y_to[s]) for s in range(2)]
    c_copy = [remote(cs.at[q], cr.at[q], send_sem.at[7 + q], c_sem.at[q], c_to[q]) for q in range(4)]
    for copy in i_copy + x_copy + y_copy + c_copy:
        copy.start()

    for copy in i_copy:
        copy.wait_recv()
    sources = jnp.concatenate([source, xinfo_r[0, 0:1], xinfo_r[1, 0:1]], axis=1)
    wide = lax.broadcasted_iota(jnp.int32, (n_tile, CELLS + 2 * LANES), 0).astype(F32)
    from_source = jnp.where(wide == sources, 1.0, 0.0).astype(jnp.bfloat16)

    rows_wait(rows_r, rows_sem)
    found = gather(rows_r[...].reshape(n_tile, LANES), from_source, 96)

    def pick(section, cut, slots):
        width = slots.shape[1]
        mask = lax.broadcasted_iota(jnp.int32, (8, width), 0).astype(F32) == slots
        return [
            jnp.sum(jnp.where(mask, found[32 * section + 8 * c:32 * section + 8 * c + 8, cut], 0.0), axis=0, keepdims=True)
            for c in range(3)
        ]

    field = pick(1, slice(0, CELLS), slot)
    near = [
        pick(2 * s, slice(CELLS + LANES * s, CELLS + LANES * (s + 1)), xinfo_r[s, 1:2]) for s in range(2)
    ]

    fields = jnp.concatenate(field + [land, jnp.zeros((4, CELLS), F32)], axis=0)
    for s in range(2):
        for part in range(2):
            cut = slice(LANES * part, LANES * (part + 1))
            edge = jnp.where(pos16 == (SIDE - 1 if s == 0 else 0), fields[:, cut], 0.0)
            for shift in (1, 2, 4, 8):
                edge = edge + roll(edge, -shift if s == 0 else shift)
            yf_s[s, :, cut] = edge
    f_copy = [remote(yf_s.at[s], yf_r.at[s], send_sem.at[11 + s], yf_sem.at[s], y_to[s]) for s in range(2)]
    for copy in f_copy:
        copy.start()

    for copy in x_copy + y_copy + c_copy:
        copy.wait_recv()

    def second(rows):
        _, slot16, pos16, first_x, first_y = masks(rows.size)
        cour = cour_ref[rows]
        x_weight = [cour * weights[i, 0:rows.size] for i in range(6)]
        y_weight = [cour * weights[6 + i, 0:rows.size] for i in range(4)]
        for q in range(4):
            sx, sy = QUADS[q]
            x_edge = [x_weight[n] * (xr[sx, n, rows] * edge_x[sx]) for n in range(3)]
            y_edge = [y_weight[2 + q % 2] * (yr[sy, q % 2, rows, cut] * edge_y[sy]) for cut in HALVES]
            for j in range(NINE):
                d = NINE * q + j
                add = [jnp.where(first_y[sy], halo_y(q, j, y_edge[half]), 0.0) for half in range(2)]
                add[sx] = add[sx] + jnp.where(first_x[sx], halo_x(q, j, x_edge[place_of(q, j)[0]]), 0.0)
                for half in range(2):
                    u0[d, rows, HALVES[half]] = u0[d, rows, HALVES[half]] + add[half]
        for sx in range(2):
            corner = [jnp.zeros((rows.size, LANES), F32)] * 3
            for q in range(4):
                if QUADS[q][0] == sx:
                    for n in range(2):
                        group = X_START[q] // 8 + n
                        corner[group] = corner[group] + edge_y[QUADS[q][1]] * cr[q, n, rows]
            for n in range(3):
                whole = xr[sx, 3 + n, rows] + x_weight[3 + n] * corner[n]
                xr[sx, 3 + n, rows] = whole * (x_weight[n] * edge_x[sx])
        for q in range(4):
            sx, sy = QUADS[q]
            for half in range(2):
                whole = yr[sy, 2 + q % 2, rows, HALVES[half]]
                if half == sx:
                    corner = jnp.where(slot16 == (0 if sx == 0 else 7), cr[q, 2, rows], 0.0)
                    whole = whole + y_weight[q % 2] * (edge_x[sx] * corner)
                yr[sy, 2 + q % 2, rows, HALVES[half]] = whole * (y_weight[2 + q % 2] * edge_y[sy])
        return ()

    each_tile(second)

    def rate_of(rows, values):
        conc, thick, floe = values
        wavelen = jnp.exp(-0.2 * (lax.broadcasted_iota(jnp.int32, (rows.size, LANES), 0) + rows.start).astype(F32))
        return decay_ref[rows] * conc * (thick + wavelen / (wavelen + floe))

    near_land = [xinfo_r[s, 2:3] for s in range(2)]

    def third(rows):
        _, slot16, pos16, first_x, first_y = masks(rows.size)
        cour = cour_ref[rows]
        factor = []
        for half in range(2):
            cut = HALVES[half]
            rate = rate_of(rows, [v[:, cut] for v in field])
            rate_ref[rows, cut] = rate
            factor.append(land[:, cut] * jnp.exp(-rate))
            factor_ref[rows, cut] = factor[half]
        zonal, merid = [0.0, 0.0], [0.0, 0.0]
        for sx in range(2):
            rim = near_land[sx] * jnp.exp(-rate_of(rows, near[sx]))
            message = [xr[sx, 3 + n, rows] * rim for n in range(3)]
            for q in range(4):
                if QUADS[q][0] != sx:
                    continue
                sy = QUADS[q][1]
                for j in range(NINE):
                    d = NINE * q + j
                    low, high = u0[d, rows, HALVES[0]] * factor[0], u0[d, rows, HALVES[1]] * factor[1]
                    cx, sn = size(q, j)
                    ax, ay = cour * cx, cour * sn
                    keep = 1.0 - cour * (cx + sn)
                    hx = halo_x(q, j, message[place_of(q, j)[0]])
                    xl, xh = moved_x(first_x, sx, ax * low, ax * high, hx, hx)
                    new = (
                        factor[0] * (keep * low + xl + ay * moved_y(first_y, sy, low)),
                        factor[1] * (keep * high + xh + ay * moved_y(first_y, sy, high)),
                    )
                    for half in range(2):
                        e0[d, rows, HALVES[half]] = new[half]
                        zonal[half] = zonal[half] + (cx if sx == 0 else -cx) * new[half]
                        merid[half] = merid[half] + (sn if sy == 0 else -sn) * new[half]
        for half in range(2):
            zonal_ref[rows, HALVES[half]] = zonal[half]
            merid_ref[rows, HALVES[half]] = merid[half]
        return ()

    each_tile(third)

    for copy in f_copy:
        copy.wait_recv()

    raw_sum = sum(math.exp(0.1 * k) for k in range(FREQS))

    def fourth(rows):
        _, _, pos16, _, first_y = masks(rows.size)
        weight_of = [weights[6 + i, 0:rows.size] for i in range(4)]
        factor = [factor_ref[rows, cut] for cut in HALVES]
        zonal = [zonal_ref[rows, cut] for cut in HALVES]
        merid = [merid_ref[rows, cut] for cut in HALVES]
        for sy in range(2):
            inner = [jnp.where(first_y[sy], f, 0.0) for f in factor]
            message = [[], []]
            for half in range(2):
                cut = HALVES[half]
                rim = yf_r[sy, 3:4, cut] * jnp.exp(-rate_of(rows, [yf_r[sy, c:c + 1, cut] for c in range(3)]))
                message[half] = [yr[sy, 2 + arr, rows, cut] * rim for arr in range(2)]
                for arr in range(2):
                    yr[sy, 2 + arr, rows, cut] = message[half][arr]
            for half in range(2):
                pair = message[half]
                sign = [1.0 if QUADS[2 * sy + arr][0] == 0 else -1.0 for arr in range(2)]
                along = sign[0] * weight_of[0] * pair[0] + sign[1] * weight_of[1] * pair[1]
                across = weight_of[2] * pair[0] + weight_of[3] * pair[1]
                if sy == 1:
                    across = -across
                for total, part in ((zonal, along), (merid, across)):
                    part = jnp.where(pos16 < NINE, part, 0.0)
                    for shift in (1, 2, 4, 8):
                        part = part + roll(part, -shift if sy == 0 else shift)
                    total[half] = total[half] + inner[half] * part
        k = lax.broadcasted_iota(jnp.int32, (rows.size, LANES), 0) + rows.start
        weight = jnp.exp(0.1 * k.astype(F32)) * (3.0 / raw_sum)
        out = []
        for scale in (None, rate_ref):
            for value in (zonal, merid):
                for half in range(2):
                    by = weight if scale is None else rate_ref[rows, HALVES[half]]
                    out.append(by * value[half])
        return out

    totals = each_tile(fourth, tuple(jnp.zeros((8, LANES), F32) for _ in range(8)))
    values = [jnp.concatenate(totals[2 * i:2 * i + 2], axis=1) * (1.0 if i < 2 else 4.0 / FREQS) for i in range(4)]
    picked = slot8.astype(F32) == slot
    lanes_of = split(jnp.concatenate([jnp.where(picked, v, 0.0) for v in values], axis=0))
    lanes_of = jnp.concatenate([lanes_of, jnp.zeros((LANES - 96, CELLS), jnp.bfloat16)], axis=0)
    table = lax.dot_general(
        from_source[:, 0:CELLS], lanes_of, (((1,), (1,)), ((), ())), preferred_element_type=F32)
    table = table + roll(table, -32) + roll(table, -64)
    back_s[...] = table.reshape(n_tile, 1, LANES)
    rows_wait(rows_s, send_sem)
    send_row(back_s, back_r, back_sem)

    def fifth(rows):
        _, _, _, _, first_y = masks(rows.size)
        for sy in range(2):
            for half in range(2):
                cut = HALVES[half]
                inner = jnp.where(first_y[sy], factor_ref[rows, cut], 0.0)
                for q in (2 * sy, 2 * sy + 1):
                    message = yr[sy, 2 + q % 2, rows, cut]
                    for j in range(NINE):
                        d = NINE * q + j
                        e0[d, rows, cut] = e0[d, rows, cut] + inner * halo_y(q, j, message)
        return ()

    each_tile(fifth)
    rows_wait(back_r, back_sem)
    rows_wait(back_s, send_sem)
    for copy in x_copy + i_copy + y_copy + c_copy + f_copy:
        copy.wait_send()


def finish(n_tile, e_ref, back_ref, route_hbm, out_hbm, coup_ref, route_in, in_sem, out_sem):
    copy = pltpu.make_async_copy(route_hbm, route_in, in_sem.at[0])
    copy.start()
    result = [
        pltpu.make_async_copy(
            e_ref.at[pl.ds(NINE * q, NINE)], out_hbm.at[pl.ds(NINE * q, NINE)], out_sem.at[q])
        for q in range(4)
    ]
    for part in result:
        part.start()
    copy.wait()
    tiles = lax.broadcasted_iota(jnp.int32, (n_tile, CELLS), 0)
    slot8 = lax.broadcasted_iota(jnp.int32, (8, CELLS), 0)
    to_dest = jnp.where(tiles == route_in[0:1], 1.0, 0.0).astype(jnp.bfloat16)
    found = gather(back_ref[...].reshape(n_tile, LANES), to_dest, 32)
    for c in range(4):
        coup_ref[c:c + 1] = jnp.sum(
            jnp.where(slot8 == route_in[1:2], found[8 * c:8 * c + 8], 0.0), axis=0, keepdims=True)
    for part in result:
        part.wait()


def solution(mesh):
    n_grp, n_tile = mesh.shape["grp"], mesh.shape["tile"]

    def body(spectrum, courant, decay, land, ice_rows, ice_route, wave_source):
        vmem = pltpu.VMEM
        dma = pltpu.SemaphoreType.DMA
        scratch = [
            vmem((DIRS, FREQS, CELLS), F32),
            vmem((1, FREQS), F32), vmem((1, FREQS), F32), vmem((SIDE, SIDE), jnp.int32),
            vmem((3, CELLS), F32), vmem((2, CELLS), jnp.int32), vmem((2, SIDE, SIDE), jnp.int32),
            vmem((10, 8, LANES), F32),
            vmem((FREQS, LANES), F32), vmem((FREQS, LANES), F32),
            vmem((FREQS, CELLS), F32), vmem((FREQS, CELLS), F32),
            vmem((FREQS, CELLS), F32), vmem((FREQS, CELLS), F32),
            vmem((2, 6, FREQS, LANES), F32), vmem((2, 6, FREQS, LANES), F32),
            vmem((2, 8, LANES), F32), vmem((2, 8, LANES), F32),
            vmem((2, 4, FREQS, CELLS), F32), vmem((2, 4, FREQS, CELLS), F32),
            vmem((4, 3, FREQS, LANES), F32), vmem((4, 3, FREQS, LANES), F32),
            vmem((2, 8, CELLS), F32), vmem((2, 8, CELLS), F32),
            vmem((n_tile, 1, LANES), F32), vmem((n_tile, 1, LANES), F32), vmem((n_tile, 1, LANES), F32),
            dma((6,)), dma((4,)), dma((13,)), dma((2,)), dma((2,)), dma((2,)), dma((4,)), dma((2,)),
            dma((1,)), dma((1,)),
        ]
        anywhere = pl.BlockSpec(memory_space=pl.ANY)
        held = pl.BlockSpec(memory_space=pltpu.VMEM)
        energy, back = pl.pallas_call(
            functools.partial(kernel, n_grp, n_tile),
            out_shape=(pltpu.VMEM((DIRS, FREQS, CELLS), F32), pltpu.VMEM((n_tile, 1, LANES), F32)),
            in_specs=[anywhere] * 7,
            out_specs=(held, held),
            scratch_shapes=scratch,
            name="coupling_step",
            compiler_params=pltpu.CompilerParams(
                collective_id=0, has_side_effects=True, vmem_limit_bytes=60 * 1024 * 1024),
        )(spectrum, courant.reshape(1, FREQS), decay.reshape(1, FREQS), land, ice_rows, ice_route, wave_source)
        return pl.pallas_call(
            functools.partial(finish, n_tile),
            out_shape=(
                jax.ShapeDtypeStruct((DIRS, FREQS, CELLS), F32),
                jax.ShapeDtypeStruct((4, CELLS), F32),
            ),
            in_specs=[held, held, anywhere],
            out_specs=(anywhere, held),
            scratch_shapes=[vmem((2, CELLS), jnp.int32), dma((1,)), dma((4,))],
            name="coupling_finish",
            compiler_params=pltpu.CompilerParams(vmem_limit_bytes=8 * 1024 * 1024),
        )(energy, back, ice_route)

    in_specs = (
        P(None, None, ("grp", "tile")),
        P(),
        P(),
        P("tile", "grp"),
        P(None, ("grp", "tile")),
        P(None, ("grp", "tile")),
        P(None, "tile", "grp"),
    )
    out_specs = (P(None, None, ("grp", "tile")), P(None, ("grp", "tile")))
    return jax.shard_map(body, mesh=mesh, in_specs=in_specs, out_specs=out_specs, check_vma=False)
```

```python
import functools
import math

import jax
import jax.numpy as jnp
from jax import lax
from jax.experimental import pallas as pl
from jax.experimental.pallas import tpu as pltpu
from jax.sharding import PartitionSpec as P

MESH = pl.DeviceIdType.MESH
F32 = jnp.float32
DIRS, FREQS, LANES, CELLS = 36, 36, 128, 256
SIDE = 16
NINE = 9
QUADS = ((0, 0), (1, 0), (1, 1), (0, 1))
X_START = (9, 0, 9, 0)
TURN = [(j + 0.5) * math.pi / 18.0 for j in range(NINE)]
HALVES = (slice(0, LANES), slice(LANES, CELLS))


def size(q, j):
    pair = math.cos(TURN[j]), math.sin(TURN[j])
    return pair if q % 2 == 0 else pair[::-1]


def place_of(q, j):
    return divmod(X_START[q] + j, 8)


def dot(a, b, dims):
    return lax.dot_general(a, b, (dims, ((), ())), precision=lax.Precision.HIGHEST, preferred_element_type=F32)


def split(value):
    high = value.astype(jnp.bfloat16)
    rest = value - high.astype(F32)
    middle = rest.astype(jnp.bfloat16)
    low = (rest - middle.astype(F32)).astype(jnp.bfloat16)
    return jnp.concatenate([high, middle, low], axis=0)


def gather(table, one_hot, rows):
    found = lax.dot_general(
        split(table.T[0:rows]), one_hot, (((1,), (0,)), ((), ())), preferred_element_type=F32)
    return found[0:rows] + found[rows:2 * rows] + found[2 * rows:]


def roll(value, shift):
    shift %= value.shape[1]
    return pltpu.roll(value, shift, 1) if shift else value


def kernel(
    n_grp, n_tile,
    spec_hbm, cour_hbm, decay_hbm, land_hbm, ice_hbm, route_hbm, source_hbm,
    e0, back_r,
    u0, cour_in, decay_in, land_in, ice_in, route_in, source_in,
    weights, cour_ref, decay_ref, factor_ref, rate_ref, zonal_ref, merid_ref,
    xs, xr, xinfo_s, xinfo_r, ys, yr, cs, cr, yf_s, yf_r,
    rows_s, rows_r, back_s,
    in_sem, spec_sem, send_sem, x_sem, xinfo_sem, y_sem, c_sem, yf_sem, rows_sem, back_sem,
):
    g = lax.axis_index("grp")
    t = lax.axis_index("tile")
    half = n_tile // 2

    def partner(n):
        step = (n + 1) // 2
        return lax.rem(t + half + jnp.where(n % 2 == 1, step, -step), n_tile)

    t_next, t_prev = lax.rem(t + 1, n_tile), lax.rem(t + n_tile - 1, n_tile)
    g_next, g_prev = lax.rem(g + 1, n_grp), lax.rem(g + n_grp - 1, n_grp)
    x_to = ((g, t_next), (g, t_prev))
    y_to = ((g_next, t), (g_prev, t))
    c_to = tuple((y_to[y][0], x_to[x][1]) for x, y in QUADS)

    barrier = pltpu.get_barrier_semaphore()

    def greet(n, carry):
        pl.semaphore_signal(barrier, inc=1, device_id=(g, partner(n)), device_id_type=MESH)
        return carry

    lax.fori_loop(0, n_tile - 1, greet, 0)
    for device in y_to + c_to:
        pl.semaphore_signal(barrier, inc=1, device_id=device, device_id_type=MESH)

    small = [
        pltpu.make_async_copy(src, dst, in_sem.at[i])
        for i, (src, dst) in enumerate((
            (ice_hbm, ice_in), (route_hbm, route_in), (cour_hbm, cour_in),
            (decay_hbm, decay_in), (land_hbm, land_in), (source_hbm, source_in),
        ))
    ]
    for copy in small:
        copy.start()
    big = [
        pltpu.make_async_copy(spec_hbm.at[pl.ds(NINE * q, NINE)], e0.at[pl.ds(NINE * q, NINE)], spec_sem.at[q])
        for q in range(4)
    ]
    for copy in big:
        copy.start()

    edge_x = (jnp.where(t > 0, 1.0, 0.0).astype(F32), jnp.where(t < n_tile - 1, 1.0, 0.0).astype(F32))
    edge_y = (jnp.where(g > 0, 1.0, 0.0).astype(F32), jnp.where(g < n_grp - 1, 1.0, 0.0).astype(F32))

    def masks(height):
        lane = lax.broadcasted_iota(jnp.int32, (height, LANES), 1)
        slot16, pos16 = lane // SIDE, lane % SIDE
        return lane, slot16, pos16, (lane < SIDE, lane >= LANES - SIDE), (pos16 == 0, pos16 == SIDE - 1)

    lane, slot16, pos16, _, _ = masks(8)

    for group in range(3):
        for kind in range(2):
            weight = jnp.zeros((8, LANES), F32)
            for q in (0, 1):
                for j in range(NINE):
                    if place_of(q, j)[0] == group:
                        weight = jnp.where(slot16 == place_of(q, j)[1], size(q, j)[kind], weight)
            weights[3 * kind + group] = weight
    for arr in range(2):
        for kind in range(2):
            weight = jnp.zeros((8, LANES), F32)
            for j in range(NINE):
                weight = jnp.where(pos16 == j, size(arr, j)[kind], weight)
            weights[6 + 2 * kind + arr] = weight

    for copy in small:
        copy.wait()

    eye = lax.broadcasted_iota(jnp.int32, (FREQS, FREQS), 0) == lax.broadcasted_iota(jnp.int32, (FREQS, FREQS), 1)

    def column(row):
        picked = jnp.where(eye, jnp.broadcast_to(row, (FREQS, FREQS)), 0.0)
        return jnp.broadcast_to(jnp.sum(picked, axis=1, keepdims=True), (FREQS, LANES))

    cour_ref[...] = column(cour_in[...])
    decay_ref[...] = column(decay_in[...])

    slot8 = lax.broadcasted_iota(jnp.int32, (8, CELLS), 0)
    tiles = lax.broadcasted_iota(jnp.int32, (n_tile, CELLS), 0)
    dest, dest_slot = route_in[0:1], route_in[1:2]
    to_dest = jnp.where(tiles == dest, 1.0, 0.0).astype(F32)
    lanes_of = jnp.concatenate(
        [jnp.where(slot8 == dest_slot, ice_in[c:c + 1], 0.0) for c in range(3)]
        + [jnp.zeros((LANES - 24, CELLS), F32)], axis=0)
    table = dot(to_dest, lanes_of, ((1,), (1,)))
    table = (
        pltpu.roll(table, 1, 0) + roll(table, 32) + roll(pltpu.roll(table, n_tile - 1, 0), 64)
    )
    rows_s[...] = table.reshape(n_tile, 1, LANES)

    cell_y = lax.broadcasted_iota(jnp.int32, (SIDE, CELLS), 1)
    row16 = lax.broadcasted_iota(jnp.int32, (SIDE, CELLS), 0)
    spread = jnp.where(cell_y % SIDE == row16, 1.0, 0.0).astype(F32)

    def flat(grid):
        wide = dot(grid.astype(F32), spread, ((1,), (0,)))
        return jnp.sum(jnp.where(cell_y // SIDE == row16, wide, 0.0), axis=0, keepdims=True)

    source, slot, land = flat(source_in[0]), flat(source_in[1]), flat(land_in[...])
    own = jnp.concatenate([source, slot, land, jnp.zeros((5, CELLS), F32)], axis=0)
    for side in range(2):
        if side == 0:
            edge = jnp.where(lane < SIDE, roll(own[:, LANES:], SIDE), 0.0)
        else:
            edge = jnp.where(lane < SIDE, own[:, :LANES], 0.0)
        for shift in (16, 32, 64):
            edge = edge + roll(edge, shift)
        xinfo_s[side] = edge

    def each_tile(body, carry=()):
        def step(n, carry):
            return tuple(a + b for a, b in zip(carry, body(pl.ds(pl.multiple_of(8 * n, 8), 8))))

        whole = FREQS // 8
        carry = lax.fori_loop(0, whole, step, carry)
        rest = body(pl.ds(8 * whole, FREQS - 8 * whole))
        return [jnp.sum(a, axis=0, keepdims=True) + jnp.sum(b, axis=0, keepdims=True) for a, b in zip(carry, rest)]

    def moved_x(first_x, sx, low, high, edge_low, edge_high):
        if sx == 0:
            rl, rh = roll(low, SIDE), roll(high, SIDE)
            return jnp.where(first_x[0], edge_low, rl), jnp.where(first_x[0], rl, rh)
        rl, rh = roll(low, -SIDE), roll(high, -SIDE)
        return jnp.where(first_x[1], rh, rl), jnp.where(first_x[1], edge_high, rh)

    def moved_y(first_y, sy, value):
        return jnp.where(first_y[sy], 0.0, roll(value, 1 if sy == 0 else -1))

    def halo_x(q, j, message):
        return roll(message, (0 if q in (0, 3) else LANES - SIDE) - SIDE * place_of(q, j)[1])

    def halo_y(q, j, message):
        return roll(message, (0 if q < 2 else SIDE - 1) - j)

    for copy in big:
        copy.wait()

    def first():
        _, slot16, pos16, first_x, first_y = masks(FREQS)
        cour = cour_ref[...]
        for q in (3, 0, 1, 2):
            sx, sy = QUADS[q]
            for j in range(NINE):
                d = NINE * q + j
                low, high = e0[d, :, HALVES[0]], e0[d, :, HALVES[1]]
                cx, sn = size(q, j)
                ax, ay = cour * cx, cour * sn
                keep = 1.0 - cour * (cx + sn)
                xl, xh = moved_x(first_x, sx, low, high, 0.0, 0.0)
                ul = keep * low + ax * xl + ay * moved_y(first_y, sy, low)
                uh = keep * high + ax * xh + ay * moved_y(first_y, sy, high)
                u0[d, :, HALVES[0]] = ul
                u0[d, :, HALVES[1]] = uh
                group, place = place_of(q, j)
                for kind, pair in enumerate(((low, high), (ul, uh))):
                    edge = roll(pair[1], SIDE * place + SIDE) if sx == 0 else roll(pair[0], SIDE * place)
                    at = 3 * kind + group
                    xs[sx, at] = jnp.where(slot16 == place, edge, xs[sx, at] if place else 0.0)
                    at = 2 * kind + q % 2
                    for half in range(2):
                        cut = HALVES[half]
                        edge = roll(pair[half], j - (SIDE - 1 if sy == 0 else 0))
                        ys[sy, at, :, cut] = jnp.where(pos16 == j, edge, ys[sy, at, :, cut] if j else 0.0)
        for q in range(4):
            sx, sy = QUADS[q]
            cs[q, 2] = roll(ys[sy, q % 2, :, HALVES[1 - sx]], SIDE if sx == 0 else -SIDE)
            for n in range(2):
                group = X_START[q] // 8 + n
                lies = [place_of(q, j)[1] for j in range(NINE) if place_of(q, j)[0] == group]
                mine = (slot16 >= lies[0]) & (slot16 <= lies[-1]) & first_y[sy]
                cs[q, n] = jnp.where(mine, roll(xs[sx, group], 1 - SIDE if sy == 0 else SIDE - 1), 0.0)

    first()

    pl.semaphore_wait(barrier, n_tile - 1 + 6)

    def send_row(src, dst, sem):
        def step(n, carry):
            d = partner(n)
            pltpu.make_async_remote_copy(
                src_ref=src.at[d], dst_ref=dst.at[t], send_sem=send_sem.at[0], recv_sem=sem.at[0],
                device_id=(g, d), device_id_type=MESH).start()
            return carry

        lax.fori_loop(0, n_tile - 1, step, 0)
        dst[pl.ds(t, 1)] = src[pl.ds(t, 1)]

    def rows_wait(ref, sem):
        view = ref.at[pl.ds(0, n_tile - 1)]
        pltpu.make_async_copy(view, view, sem.at[0]).wait()

    send_row(rows_s, rows_r, rows_sem)

    def remote(src, dst, sent, arrived, device):
        return pltpu.make_async_remote_copy(
            src_ref=src, dst_ref=dst, send_sem=sent, recv_sem=arrived, device_id=device, device_id_type=MESH)

    x_copy = [remote(xs.at[s], xr.at[s], send_sem.at[1 + s], x_sem.at[s], x_to[s]) for s in range(2)]
    i_copy = [remote(xinfo_s.at[s], xinfo_r.at[s], send_sem.at[3 + s], xinfo_sem.at[s], x_to[s]) for s in range(2)]
    y_copy = [remote(ys.at[s], yr.at[s], send_sem.at[5 + s], y_sem.at[s], y_to[s]) for s in range(2)]
    c_copy = [remote(cs.at[q], cr.at[q], send_sem.at[7 + q], c_sem.at[q], c_to[q]) for q in range(4)]
    for copy in i_copy + x_copy + y_copy + c_copy:
        copy.start()

    for copy in i_copy:
        copy.wait_recv()
    sources = jnp.concatenate([source, xinfo_r[0, 0:1], xinfo_r[1, 0:1]], axis=1)
    wide = lax.broadcasted_iota(jnp.int32, (n_tile, CELLS + 2 * LANES), 0).astype(F32)
    from_source = jnp.where(wide == sources, 1.0, 0.0).astype(jnp.bfloat16)

    rows_wait(rows_r, rows_sem)
    found = gather(rows_r[...].reshape(n_tile, LANES), from_source, 96)

    def pick(section, cut, slots):
        width = slots.shape[1]
        mask = lax.broadcasted_iota(jnp.int32, (8, width), 0).astype(F32) == slots
        return [
            jnp.sum(jnp.where(mask, found[32 * section + 8 * c:32 * section + 8 * c + 8, cut], 0.0), axis=0, keepdims=True)
            for c in range(3)
        ]

    field = pick(1, slice(0, CELLS), slot)
    near = [
        pick(2 * s, slice(CELLS + LANES * s, CELLS + LANES * (s + 1)), xinfo_r[s, 1:2]) for s in range(2)
    ]

    fields = jnp.concatenate(field + [land, jnp.zeros((4, CELLS), F32)], axis=0)
    for s in range(2):
        for part in range(2):
            cut = slice(LANES * part, LANES * (part + 1))
            edge = jnp.where(pos16 == (SIDE - 1 if s == 0 else 0), fields[:, cut], 0.0)
            for shift in (1, 2, 4, 8):
                edge = edge + roll(edge, -shift if s == 0 else shift)
            yf_s[s, :, cut] = edge
    f_copy = [remote(yf_s.at[s], yf_r.at[s], send_sem.at[11 + s], yf_sem.at[s], y_to[s]) for s in range(2)]
    for copy in f_copy:
        copy.start()

    for copy in x_copy + y_copy + c_copy:
        copy.wait_recv()

    def second(rows):
        _, slot16, pos16, first_x, first_y = masks(rows.size)
        cour = cour_ref[rows]
        x_weight = [cour * weights[i, 0:rows.size] for i in range(6)]
        y_weight = [cour * weights[6 + i, 0:rows.size] for i in range(4)]
        for q in range(4):
            sx, sy = QUADS[q]
            x_edge = [x_weight[n] * (xr[sx, n, rows] * edge_x[sx]) for n in range(3)]
            y_edge = [y_weight[2 + q % 2] * (yr[sy, q % 2, rows, cut] * edge_y[sy]) for cut in HALVES]
            for j in range(NINE):
                d = NINE * q + j
                add = [jnp.where(first_y[sy], halo_y(q, j, y_edge[half]), 0.0) for half in range(2)]
                add[sx] = add[sx] + jnp.where(first_x[sx], halo_x(q, j, x_edge[place_of(q, j)[0]]), 0.0)
                for half in range(2):
                    u0[d, rows, HALVES[half]] = u0[d, rows, HALVES[half]] + add[half]
        for sx in range(2):
            corner = [jnp.zeros((rows.size, LANES), F32)] * 3
            for q in range(4):
                if QUADS[q][0] == sx:
                    for n in range(2):
                        group = X_START[q] // 8 + n
                        corner[group] = corner[group] + edge_y[QUADS[q][1]] * cr[q, n, rows]
            for n in range(3):
                whole = xr[sx, 3 + n, rows] + x_weight[3 + n] * corner[n]
                xr[sx, 3 + n, rows] = whole * (x_weight[n] * edge_x[sx])
        for q in range(4):
            sx, sy = QUADS[q]
            for half in range(2):
                whole = yr[sy, 2 + q % 2, rows, HALVES[half]]
                if half == sx:
                    corner = jnp.where(slot16 == (0 if sx == 0 else 7), cr[q, 2, rows], 0.0)
                    whole = whole + y_weight[q % 2] * (edge_x[sx] * corner)
                yr[sy, 2 + q % 2, rows, HALVES[half]] = whole * (y_weight[2 + q % 2] * edge_y[sy])
        return ()

    each_tile(second)

    def rate_of(rows, values):
        conc, thick, floe = values
        wavelen = jnp.exp(-0.2 * (lax.broadcasted_iota(jnp.int32, (rows.size, LANES), 0) + rows.start).astype(F32))
        return decay_ref[rows] * conc * (thick + wavelen / (wavelen + floe))

    near_land = [xinfo_r[s, 2:3] for s in range(2)]

    def third(rows):
        _, slot16, pos16, first_x, first_y = masks(rows.size)
        cour = cour_ref[rows]
        factor = []
        for half in range(2):
            cut = HALVES[half]
            rate = rate_of(rows, [v[:, cut] for v in field])
            rate_ref[rows, cut] = rate
            factor.append(land[:, cut] * jnp.exp(-rate))
            factor_ref[rows, cut] = factor[half]
        zonal, merid = [0.0, 0.0], [0.0, 0.0]
        for sx in range(2):
            rim = near_land[sx] * jnp.exp(-rate_of(rows, near[sx]))
            message = [xr[sx, 3 + n, rows] * rim for n in range(3)]
            for q in range(4):
                if QUADS[q][0] != sx:
                    continue
                sy = QUADS[q][1]
                for j in range(NINE):
                    d = NINE * q + j
                    low, high = u0[d, rows, HALVES[0]] * factor[0], u0[d, rows, HALVES[1]] * factor[1]
                    cx, sn = size(q, j)
                    ax, ay = cour * cx, cour * sn
                    keep = 1.0 - cour * (cx + sn)
                    hx = halo_x(q, j, message[place_of(q, j)[0]])
                    xl, xh = moved_x(first_x, sx, ax * low, ax * high, hx, hx)
                    new = (
                        factor[0] * (keep * low + xl + ay * moved_y(first_y, sy, low)),
                        factor[1] * (keep * high + xh + ay * moved_y(first_y, sy, high)),
                    )
                    for half in range(2):
                        e0[d, rows, HALVES[half]] = new[half]
                        zonal[half] = zonal[half] + (cx if sx == 0 else -cx) * new[half]
                        merid[half] = merid[half] + (sn if sy == 0 else -sn) * new[half]
        for half in range(2):
            zonal_ref[rows, HALVES[half]] = zonal[half]
            merid_ref[rows, HALVES[half]] = merid[half]
        return ()

    each_tile(third)

    for copy in f_copy:
        copy.wait_recv()

    raw_sum = sum(math.exp(0.1 * k) for k in range(FREQS))

    def fourth(rows):
        _, _, pos16, _, first_y = masks(rows.size)
        weight_of = [weights[6 + i, 0:1] for i in range(4)]
        factor = [factor_ref[rows, cut] for cut in HALVES]
        zonal = [zonal_ref[rows, cut] for cut in HALVES]
        merid = [merid_ref[rows, cut] for cut in HALVES]
        for sy in range(2):
            inner = [jnp.where(first_y[sy], f, 0.0) for f in factor]
            message = [[], []]
            for half in range(2):
                cut = HALVES[half]
                rim = yf_r[sy, 3:4, cut] * jnp.exp(-rate_of(rows, [yf_r[sy, c:c + 1, cut] for c in range(3)]))
                message[half] = [yr[sy, 2 + arr, rows, cut] * rim for arr in range(2)]
                for arr in range(2):
                    yr[sy, 2 + arr, rows, cut] = message[half][arr]
            for half in range(2):
                pair = message[half]
                sign = [1.0 if QUADS[2 * sy + arr][0] == 0 else -1.0 for arr in range(2)]
                along = sign[0] * weight_of[0] * pair[0] + sign[1] * weight_of[1] * pair[1]
                across = weight_of[2] * pair[0] + weight_of[3] * pair[1]
                if sy == 1:
                    across = -across
                for total, part in ((zonal, along), (merid, across)):
                    part = jnp.where(pos16 < NINE, part, 0.0)
                    for shift in (1, 2, 4, 8):
                        part = part + roll(part, -shift if sy == 0 else shift)
                    total[half] = total[half] + inner[half] * part
        k = lax.broadcasted_iota(jnp.int32, (rows.size, LANES), 0) + rows.start
        weight = jnp.exp(0.1 * k.astype(F32)) * (3.0 / raw_sum)
        out = []
        for scale in (None, rate_ref):
            for value in (zonal, merid):
                for half in range(2):
                    by = weight if scale is None else rate_ref[rows, HALVES[half]]
                    out.append(by * value[half])
        return out

    totals = [jnp.sum(v, axis=0, keepdims=True) for v in fourth(pl.ds(0, FREQS))]
    values = [jnp.concatenate(totals[2 * i:2 * i + 2], axis=1) * (1.0 if i < 2 else 4.0 / FREQS) for i in range(4)]
    picked = slot8.astype(F32) == slot
    lanes_of = split(jnp.concatenate([jnp.where(picked, v, 0.0) for v in values], axis=0))
    lanes_of = jnp.concatenate([lanes_of, jnp.zeros((LANES - 96, CELLS), jnp.bfloat16)], axis=0)
    table = lax.dot_general(
        from_source[:, 0:CELLS], lanes_of, (((1,), (1,)), ((), ())), preferred_element_type=F32)
    table = table + roll(table, -32) + roll(table, -64)
    back_s[...] = table.reshape(n_tile, 1, LANES)
    rows_wait(rows_s, send_sem)
    send_row(back_s, back_r, back_sem)

    def fifth(rows):
        _, _, _, _, first_y = masks(rows.size)
        for sy in range(2):
            for half in range(2):
                cut = HALVES[half]
                inner = jnp.where(first_y[sy], factor_ref[rows, cut], 0.0)
                for q in (2 * sy, 2 * sy + 1):
                    message = yr[sy, 2 + q % 2, rows, cut]
                    for j in range(NINE):
                        d = NINE * q + j
                        e0[d, rows, cut] = e0[d, rows, cut] + inner * halo_y(q, j, message)
        return ()

    each_tile(fifth)
    rows_wait(back_r, back_sem)
    rows_wait(back_s, send_sem)
    for copy in x_copy + i_copy + y_copy + c_copy + f_copy:
        copy.wait_send()


def finish(n_tile, e_ref, back_ref, route_hbm, out_hbm, coup_ref, route_in, in_sem, out_sem):
    copy = pltpu.make_async_copy(route_hbm, route_in, in_sem.at[0])
    copy.start()
    result = [
        pltpu.make_async_copy(
            e_ref.at[pl.ds(NINE * q, NINE)], out_hbm.at[pl.ds(NINE * q, NINE)], out_sem.at[q])
        for q in range(4)
    ]
    for part in result:
        part.start()
    copy.wait()
    tiles = lax.broadcasted_iota(jnp.int32, (n_tile, CELLS), 0)
    slot8 = lax.broadcasted_iota(jnp.int32, (8, CELLS), 0)
    to_dest = jnp.where(tiles == route_in[0:1], 1.0, 0.0).astype(jnp.bfloat16)
    found = gather(back_ref[...].reshape(n_tile, LANES), to_dest, 32)
    for c in range(4):
        coup_ref[c:c + 1] = jnp.sum(
            jnp.where(slot8 == route_in[1:2], found[8 * c:8 * c + 8], 0.0), axis=0, keepdims=True)
    for part in result:
        part.wait()


def solution(mesh):
    n_grp, n_tile = mesh.shape["grp"], mesh.shape["tile"]

    def body(spectrum, courant, decay, land, ice_rows, ice_route, wave_source):
        vmem = pltpu.VMEM
        dma = pltpu.SemaphoreType.DMA
        scratch = [
            vmem((DIRS, FREQS, CELLS), F32),
            vmem((1, FREQS), F32), vmem((1, FREQS), F32), vmem((SIDE, SIDE), jnp.int32),
            vmem((3, CELLS), F32), vmem((2, CELLS), jnp.int32), vmem((2, SIDE, SIDE), jnp.int32),
            vmem((10, 8, LANES), F32),
            vmem((FREQS, LANES), F32), vmem((FREQS, LANES), F32),
            vmem((FREQS, CELLS), F32), vmem((FREQS, CELLS), F32),
            vmem((FREQS, CELLS), F32), vmem((FREQS, CELLS), F32),
            vmem((2, 6, FREQS, LANES), F32), vmem((2, 6, FREQS, LANES), F32),
            vmem((2, 8, LANES), F32), vmem((2, 8, LANES), F32),
            vmem((2, 4, FREQS, CELLS), F32), vmem((2, 4, FREQS, CELLS), F32),
            vmem((4, 3, FREQS, LANES), F32), vmem((4, 3, FREQS, LANES), F32),
            vmem((2, 8, CELLS), F32), vmem((2, 8, CELLS), F32),
            vmem((n_tile, 1, LANES), F32), vmem((n_tile, 1, LANES), F32), vmem((n_tile, 1, LANES), F32),
            dma((6,)), dma((4,)), dma((13,)), dma((2,)), dma((2,)), dma((2,)), dma((4,)), dma((2,)),
            dma((1,)), dma((1,)),
        ]
        anywhere = pl.BlockSpec(memory_space=pl.ANY)
        held = pl.BlockSpec(memory_space=pltpu.VMEM)
        energy, back = pl.pallas_call(
            functools.partial(kernel, n_grp, n_tile),
            out_shape=(pltpu.VMEM((DIRS, FREQS, CELLS), F32), pltpu.VMEM((n_tile, 1, LANES), F32)),
            in_specs=[anywhere] * 7,
            out_specs=(held, held),
            scratch_shapes=scratch,
            name="coupling_step",
            compiler_params=pltpu.CompilerParams(
                collective_id=0, has_side_effects=True, vmem_limit_bytes=60 * 1024 * 1024),
        )(spectrum, courant.reshape(1, FREQS), decay.reshape(1, FREQS), land, ice_rows, ice_route, wave_source)
        return pl.pallas_call(
            functools.partial(finish, n_tile),
            out_shape=(
                jax.ShapeDtypeStruct((DIRS, FREQS, CELLS), F32),
                jax.ShapeDtypeStruct((4, CELLS), F32),
            ),
            in_specs=[held, held, anywhere],
            out_specs=(anywhere, held),
            scratch_shapes=[vmem((2, CELLS), jnp.int32), dma((1,)), dma((4,))],
            name="coupling_finish",
            compiler_params=pltpu.CompilerParams(vmem_limit_bytes=8 * 1024 * 1024),
        )(energy, back, ice_route)

    in_specs = (
        P(None, None, ("grp", "tile")),
        P(),
        P(),
        P("tile", "grp"),
        P(None, ("grp", "tile")),
        P(None, ("grp", "tile")),
        P(None, "tile", "grp"),
    )
    out_specs = (P(None, None, ("grp", "tile")), P(None, ("grp", "tile")))
    return jax.shard_map(body, mesh=mesh, in_specs=in_specs, out_specs=out_specs, check_vma=False)
```

```python
import functools
import math

import jax
import jax.numpy as jnp
from jax import lax
from jax.experimental import pallas as pl
from jax.experimental.pallas import tpu as pltpu
from jax.sharding import PartitionSpec as P

MESH = pl.DeviceIdType.MESH
F32 = jnp.float32
DIRS, FREQS, LANES, CELLS = 36, 36, 128, 256
SIDE = 16
NINE = 9
QUADS = ((0, 0), (1, 0), (1, 1), (0, 1))
X_START = (9, 0, 9, 0)
TURN = [(j + 0.5) * math.pi / 18.0 for j in range(NINE)]
HALVES = (slice(0, LANES), slice(LANES, CELLS))


def size(q, j):
    pair = math.cos(TURN[j]), math.sin(TURN[j])
    return pair if q % 2 == 0 else pair[::-1]


def place_of(q, j):
    return divmod(X_START[q] + j, 8)


def dot(a, b, dims):
    return lax.dot_general(a, b, (dims, ((), ())), precision=lax.Precision.HIGHEST, preferred_element_type=F32)


def split(value):
    high = value.astype(jnp.bfloat16)
    rest = value - high.astype(F32)
    middle = rest.astype(jnp.bfloat16)
    low = (rest - middle.astype(F32)).astype(jnp.bfloat16)
    return jnp.concatenate([high, middle, low], axis=0)


def gather(table, one_hot, rows):
    found = lax.dot_general(
        split(table.T[0:rows]), one_hot, (((1,), (0,)), ((), ())), preferred_element_type=F32)
    return found[0:rows] + found[rows:2 * rows] + found[2 * rows:]


def roll(value, shift):
    shift %= value.shape[1]
    return pltpu.roll(value, shift, 1) if shift else value


def kernel(
    n_grp, n_tile,
    spec_hbm, cour_hbm, decay_hbm, land_hbm, ice_hbm, route_hbm, source_hbm,
    e0, back_r,
    u0, cour_in, decay_in, land_in, ice_in, route_in, source_in,
    weights, cour_ref, decay_ref, factor_ref, rate_ref, zonal_ref, merid_ref,
    xs, xr, xinfo_s, xinfo_r, ys, yr, cs, cr, yf_s, yf_r,
    rows_s, rows_r, back_s,
    in_sem, spec_sem, send_sem, x_sem, xinfo_sem, y_sem, c_sem, yf_sem, rows_sem, back_sem,
):
    g = lax.axis_index("grp")
    t = lax.axis_index("tile")
    half = n_tile // 2

    def partner(n):
        step = (n + 1) // 2
        return lax.rem(t + half + jnp.where(n % 2 == 1, step, -step), n_tile)

    t_next, t_prev = lax.rem(t + 1, n_tile), lax.rem(t + n_tile - 1, n_tile)
    g_next, g_prev = lax.rem(g + 1, n_grp), lax.rem(g + n_grp - 1, n_grp)
    x_to = ((g, t_next), (g, t_prev))
    y_to = ((g_next, t), (g_prev, t))
    c_to = tuple((y_to[y][0], x_to[x][1]) for x, y in QUADS)

    barrier = pltpu.get_barrier_semaphore()

    def greet(n, carry):
        pl.semaphore_signal(barrier, inc=1, device_id=(g, partner(n)), device_id_type=MESH)
        return carry

    lax.fori_loop(0, n_tile - 1, greet, 0)
    for device in y_to + c_to:
        pl.semaphore_signal(barrier, inc=1, device_id=device, device_id_type=MESH)

    small = [
        pltpu.make_async_copy(src, dst, in_sem.at[i])
        for i, (src, dst) in enumerate((
            (ice_hbm, ice_in), (route_hbm, route_in), (cour_hbm, cour_in),
            (decay_hbm, decay_in), (land_hbm, land_in), (source_hbm, source_in),
        ))
    ]
    for copy in small:
        copy.start()
    big = [
        pltpu.make_async_copy(spec_hbm.at[pl.ds(NINE * q, NINE)], e0.at[pl.ds(NINE * q, NINE)], spec_sem.at[q])
        for q in range(4)
    ]
    for copy in big:
        copy.start()

    edge_x = (jnp.where(t > 0, 1.0, 0.0).astype(F32), jnp.where(t < n_tile - 1, 1.0, 0.0).astype(F32))
    edge_y = (jnp.where(g > 0, 1.0, 0.0).astype(F32), jnp.where(g < n_grp - 1, 1.0, 0.0).astype(F32))

    def masks(height):
        lane = lax.broadcasted_iota(jnp.int32, (height, LANES), 1)
        slot16, pos16 = lane // SIDE, lane % SIDE
        return lane, slot16, pos16, (lane < SIDE, lane >= LANES - SIDE), (pos16 == 0, pos16 == SIDE - 1)

    lane, slot16, pos16, _, _ = masks(8)

    for group in range(3):
        for kind in range(2):
            weight = jnp.zeros((8, LANES), F32)
            for q in (0, 1):
                for j in range(NINE):
                    if place_of(q, j)[0] == group:
                        weight = jnp.where(slot16 == place_of(q, j)[1], size(q, j)[kind], weight)
            weights[3 * kind + group] = weight
    for arr in range(2):
        for kind in range(2):
            weight = jnp.zeros((8, LANES), F32)
            for j in range(NINE):
                weight = jnp.where(pos16 == j, size(arr, j)[kind], weight)
            weights[6 + 2 * kind + arr] = weight

    for copy in small:
        copy.wait()

    eye = lax.broadcasted_iota(jnp.int32, (FREQS, FREQS), 0) == lax.broadcasted_iota(jnp.int32, (FREQS, FREQS), 1)

    def column(row):
        picked = jnp.where(eye, jnp.broadcast_to(row, (FREQS, FREQS)), 0.0)
        return jnp.broadcast_to(jnp.sum(picked, axis=1, keepdims=True), (FREQS, LANES))

    cour_ref[...] = column(cour_in[...])
    decay_ref[...] = column(decay_in[...])

    slot8 = lax.broadcasted_iota(jnp.int32, (8, CELLS), 0)
    tiles = lax.broadcasted_iota(jnp.int32, (n_tile, CELLS), 0)
    dest, dest_slot = route_in[0:1], route_in[1:2]
    to_dest = jnp.where(tiles == dest, 1.0, 0.0).astype(F32)
    lanes_of = jnp.concatenate(
        [jnp.where(slot8 == dest_slot, ice_in[c:c + 1], 0.0) for c in range(3)]
        + [jnp.zeros((LANES - 24, CELLS), F32)], axis=0)
    table = dot(to_dest, lanes_of, ((1,), (1,)))
    table = (
        pltpu.roll(table, 1, 0) + roll(table, 32) + roll(pltpu.roll(table, n_tile - 1, 0), 64)
    )
    rows_s[...] = table.reshape(n_tile, 1, LANES)

    cell_y = lax.broadcasted_iota(jnp.int32, (SIDE, CELLS), 1)
    row16 = lax.broadcasted_iota(jnp.int32, (SIDE, CELLS), 0)
    spread = jnp.where(cell_y % SIDE == row16, 1.0, 0.0).astype(F32)

    def flat(grid):
        wide = dot(grid.astype(F32), spread, ((1,), (0,)))
        return jnp.sum(jnp.where(cell_y // SIDE == row16, wide, 0.0), axis=0, keepdims=True)

    source, slot, land = flat(source_in[0]), flat(source_in[1]), flat(land_in[...])
    own = jnp.concatenate([source, slot, land, jnp.zeros((5, CELLS), F32)], axis=0)
    for side in range(2):
        if side == 0:
            edge = jnp.where(lane < SIDE, roll(own[:, LANES:], SIDE), 0.0)
        else:
            edge = jnp.where(lane < SIDE, own[:, :LANES], 0.0)
        for shift in (16, 32, 64):
            edge = edge + roll(edge, shift)
        xinfo_s[side] = edge

    def each_tile(body, carry=()):
        def step(n, carry):
            return tuple(a + b for a, b in zip(carry, body(pl.ds(pl.multiple_of(8 * n, 8), 8))))

        whole = FREQS // 8
        carry = lax.fori_loop(0, whole, step, carry)
        rest = body(pl.ds(8 * whole, FREQS - 8 * whole))
        return [jnp.sum(a, axis=0, keepdims=True) + jnp.sum(b, axis=0, keepdims=True) for a, b in zip(carry, rest)]

    def moved_x(first_x, sx, low, high, edge_low, edge_high):
        if sx == 0:
            rl, rh = roll(low, SIDE), roll(high, SIDE)
            return jnp.where(first_x[0], edge_low, rl), jnp.where(first_x[0], rl, rh)
        rl, rh = roll(low, -SIDE), roll(high, -SIDE)
        return jnp.where(first_x[1], rh, rl), jnp.where(first_x[1], edge_high, rh)

    def moved_y(first_y, sy, value):
        return jnp.where(first_y[sy], 0.0, roll(value, 1 if sy == 0 else -1))

    def halo_x(q, j, message):
        return roll(message, (0 if q in (0, 3) else LANES - SIDE) - SIDE * place_of(q, j)[1])

    def halo_y(q, j, message):
        return roll(message, (0 if q < 2 else SIDE - 1) - j)

    for copy in big:
        copy.wait()

    def first():
        _, slot16, pos16, first_x, first_y = masks(FREQS)
        cour = cour_ref[...]
        for q in (3, 0, 1, 2):
            sx, sy = QUADS[q]
            for j in range(NINE):
                d = NINE * q + j
                low, high = e0[d, :, HALVES[0]], e0[d, :, HALVES[1]]
                cx, sn = size(q, j)
                ax, ay = cour * cx, cour * sn
                keep = 1.0 - cour * (cx + sn)
                xl, xh = moved_x(first_x, sx, low, high, 0.0, 0.0)
                ul = keep * low + ax * xl + ay * moved_y(first_y, sy, low)
                uh = keep * high + ax * xh + ay * moved_y(first_y, sy, high)
                u0[d, :, HALVES[0]] = ul
                u0[d, :, HALVES[1]] = uh
                group, place = place_of(q, j)
                for kind, pair in enumerate(((low, high), (ul, uh))):
                    edge = roll(pair[1], SIDE * place + SIDE) if sx == 0 else roll(pair[0], SIDE * place)
                    at = 3 * kind + group
                    xs[sx, at] = jnp.where(slot16 == place, edge, xs[sx, at] if place else 0.0)
                    at = 2 * kind + q % 2
                    for half in range(2):
                        cut = HALVES[half]
                        edge = roll(pair[half], j - (SIDE - 1 if sy == 0 else 0))
                        ys[sy, at, :, cut] = jnp.where(pos16 == j, edge, ys[sy, at, :, cut] if j else 0.0)
        for q in range(4):
            sx, sy = QUADS[q]
            cs[q, 2] = roll(ys[sy, q % 2, :, HALVES[1 - sx]], SIDE if sx == 0 else -SIDE)
            for n in range(2):
                group = X_START[q] // 8 + n
                lies = [place_of(q, j)[1] for j in range(NINE) if place_of(q, j)[0] == group]
                mine = (slot16 >= lies[0]) & (slot16 <= lies[-1]) & first_y[sy]
                cs[q, n] = jnp.where(mine, roll(xs[sx, group], 1 - SIDE if sy == 0 else SIDE - 1), 0.0)

    first()

    pl.semaphore_wait(barrier, n_tile - 1 + 6)

    def send_row(src, dst, sem):
        def step(n, carry):
            d = partner(n)
            pltpu.make_async_remote_copy(
                src_ref=src.at[d], dst_ref=dst.at[t], send_sem=send_sem.at[0], recv_sem=sem.at[0],
                device_id=(g, d), device_id_type=MESH).start()
            return carry

        lax.fori_loop(0, n_tile - 1, step, 0)
        dst[pl.ds(t, 1)] = src[pl.ds(t, 1)]

    def rows_wait(ref, sem):
        view = ref.at[pl.ds(0, n_tile - 1)]
        pltpu.make_async_copy(view, view, sem.at[0]).wait()

    send_row(rows_s, rows_r, rows_sem)

    def remote(src, dst, sent, arrived, device):
        return pltpu.make_async_remote_copy(
            src_ref=src, dst_ref=dst, send_sem=sent, recv_sem=arrived, device_id=device, device_id_type=MESH)

    x_copy = [remote(xs.at[s], xr.at[s], send_sem.at[1 + s], x_sem.at[s], x_to[s]) for s in range(2)]
    i_copy = [remote(xinfo_s.at[s], xinfo_r.at[s], send_sem.at[3 + s], xinfo_sem.at[s], x_to[s]) for s in range(2)]
    y_copy = [remote(ys.at[s], yr.at[s], send_sem.at[5 + s], y_sem.at[s], y_to[s]) for s in range(2)]
    c_copy = [remote(cs.at[q], cr.at[q], send_sem.at[7 + q], c_sem.at[q], c_to[q]) for q in range(4)]
    for copy in i_copy + x_copy + y_copy + c_copy:
        copy.start()

    for copy in i_copy:
        copy.wait_recv()
    sources = jnp.concatenate([source, xinfo_r[0, 0:1], xinfo_r[1, 0:1]], axis=1)
    wide = lax.broadcasted_iota(jnp.int32, (n_tile, CELLS + 2 * LANES), 0).astype(F32)
    from_source = jnp.where(wide == sources, 1.0, 0.0).astype(jnp.bfloat16)

    rows_wait(rows_r, rows_sem)
    found = gather(rows_r[...].reshape(n_tile, LANES), from_source, 96)

    def pick(section, cut, slots):
        width = slots.shape[1]
        mask = lax.broadcasted_iota(jnp.int32, (8, width), 0).astype(F32) == slots
        return [
            jnp.sum(jnp.where(mask, found[32 * section + 8 * c:32 * section + 8 * c + 8, cut], 0.0), axis=0, keepdims=True)
            for c in range(3)
        ]

    field = pick(1, slice(0, CELLS), slot)
    near = [
        pick(2 * s, slice(CELLS + LANES * s, CELLS + LANES * (s + 1)), xinfo_r[s, 1:2]) for s in range(2)
    ]

    fields = jnp.concatenate(field + [land, jnp.zeros((4, CELLS), F32)], axis=0)
    for s in range(2):
        for part in range(2):
            cut = slice(LANES * part, LANES * (part + 1))
            edge = jnp.where(pos16 == (SIDE - 1 if s == 0 else 0), fields[:, cut], 0.0)
            for shift in (1, 2, 4, 8):
                edge = edge + roll(edge, -shift if s == 0 else shift)
            yf_s[s, :, cut] = edge
    f_copy = [remote(yf_s.at[s], yf_r.at[s], send_sem.at[11 + s], yf_sem.at[s], y_to[s]) for s in range(2)]
    for copy in f_copy:
        copy.start()

    for copy in x_copy + y_copy + c_copy:
        copy.wait_recv()

    def second(rows):
        _, slot16, pos16, first_x, first_y = masks(rows.size)
        cour = cour_ref[rows]
        x_weight = [cour * weights[i, 0:1] for i in range(6)]
        y_weight = [cour * weights[6 + i, 0:1] for i in range(4)]
        for q in range(4):
            sx, sy = QUADS[q]
            x_edge = [x_weight[n] * (xr[sx, n, rows] * edge_x[sx]) for n in range(3)]
            y_edge = [y_weight[2 + q % 2] * (yr[sy, q % 2, rows, cut] * edge_y[sy]) for cut in HALVES]
            for j in range(NINE):
                d = NINE * q + j
                add = [jnp.where(first_y[sy], halo_y(q, j, y_edge[half]), 0.0) for half in range(2)]
                add[sx] = add[sx] + jnp.where(first_x[sx], halo_x(q, j, x_edge[place_of(q, j)[0]]), 0.0)
                for half in range(2):
                    u0[d, rows, HALVES[half]] = u0[d, rows, HALVES[half]] + add[half]
        for sx in range(2):
            corner = [jnp.zeros((rows.size, LANES), F32)] * 3
            for q in range(4):
                if QUADS[q][0] == sx:
                    for n in range(2):
                        group = X_START[q] // 8 + n
                        corner[group] = corner[group] + edge_y[QUADS[q][1]] * cr[q, n, rows]
            for n in range(3):
                whole = xr[sx, 3 + n, rows] + x_weight[3 + n] * corner[n]
                xr[sx, 3 + n, rows] = whole * (x_weight[n] * edge_x[sx])
        for q in range(4):
            sx, sy = QUADS[q]
            for half in range(2):
                whole = yr[sy, 2 + q % 2, rows, HALVES[half]]
                if half == sx:
                    corner = jnp.where(slot16 == (0 if sx == 0 else 7), cr[q, 2, rows], 0.0)
                    whole = whole + y_weight[q % 2] * (edge_x[sx] * corner)
                yr[sy, 2 + q % 2, rows, HALVES[half]] = whole * (y_weight[2 + q % 2] * edge_y[sy])
        return ()

    second(pl.ds(0, FREQS))

    def rate_of(rows, values):
        conc, thick, floe = values
        wavelen = jnp.exp(-0.2 * (lax.broadcasted_iota(jnp.int32, (rows.size, LANES), 0) + rows.start).astype(F32))
        return decay_ref[rows] * conc * (thick + wavelen / (wavelen + floe))

    near_land = [xinfo_r[s, 2:3] for s in range(2)]

    def third(rows):
        _, slot16, pos16, first_x, first_y = masks(rows.size)
        cour = cour_ref[rows]
        factor = []
        for half in range(2):
            cut = HALVES[half]
            rate = rate_of(rows, [v[:, cut] for v in field])
            rate_ref[rows, cut] = rate
            factor.append(land[:, cut] * jnp.exp(-rate))
            factor_ref[rows, cut] = factor[half]
        zonal, merid = [0.0, 0.0], [0.0, 0.0]
        for sx in range(2):
            rim = near_land[sx] * jnp.exp(-rate_of(rows, near[sx]))
            message = [xr[sx, 3 + n, rows] * rim for n in range(3)]
            for q in range(4):
                if QUADS[q][0] != sx:
                    continue
                sy = QUADS[q][1]
                for j in range(NINE):
                    d = NINE * q + j
                    low, high = u0[d, rows, HALVES[0]] * factor[0], u0[d, rows, HALVES[1]] * factor[1]
                    cx, sn = size(q, j)
                    ax, ay = cour * cx, cour * sn
                    keep = 1.0 - cour * (cx + sn)
                    hx = halo_x(q, j, message[place_of(q, j)[0]])
                    xl, xh = moved_x(first_x, sx, ax * low, ax * high, hx, hx)
                    new = (
                        factor[0] * (keep * low + xl + ay * moved_y(first_y, sy, low)),
                        factor[1] * (keep * high + xh + ay * moved_y(first_y, sy, high)),
                    )
                    for half in range(2):
                        e0[d, rows, HALVES[half]] = new[half]
                        zonal[half] = zonal[half] + (cx if sx == 0 else -cx) * new[half]
                        merid[half] = merid[half] + (sn if sy == 0 else -sn) * new[half]
        for half in range(2):
            zonal_ref[rows, HALVES[half]] = zonal[half]
            merid_ref[rows, HALVES[half]] = merid[half]
        return ()

    each_tile(third)

    for copy in f_copy:
        copy.wait_recv()

    raw_sum = sum(math.exp(0.1 * k) for k in range(FREQS))

    def fourth(rows):
        _, _, pos16, _, first_y = masks(rows.size)
        weight_of = [weights[6 + i, 0:1] for i in range(4)]
        factor = [factor_ref[rows, cut] for cut in HALVES]
        zonal = [zonal_ref[rows, cut] for cut in HALVES]
        merid = [merid_ref[rows, cut] for cut in HALVES]
        for sy in range(2):
            inner = [jnp.where(first_y[sy], f, 0.0) for f in factor]
            message = [[], []]
            for half in range(2):
                cut = HALVES[half]
                rim = yf_r[sy, 3:4, cut] * jnp.exp(-rate_of(rows, [yf_r[sy, c:c + 1, cut] for c in range(3)]))
                message[half] = [yr[sy, 2 + arr, rows, cut] * rim for arr in range(2)]
                for arr in range(2):
                    yr[sy, 2 + arr, rows, cut] = message[half][arr]
            for half in range(2):
                pair = message[half]
                sign = [1.0 if QUADS[2 * sy + arr][0] == 0 else -1.0 for arr in range(2)]
                along = sign[0] * weight_of[0] * pair[0] + sign[1] * weight_of[1] * pair[1]
                across = weight_of[2] * pair[0] + weight_of[3] * pair[1]
                if sy == 1:
                    across = -across
                for total, part in ((zonal, along), (merid, across)):
                    part = jnp.where(pos16 < NINE, part, 0.0)
                    for shift in (1, 2, 4, 8):
                        part = part + roll(part, -shift if sy == 0 else shift)
                    total[half] = total[half] + inner[half] * part
        k = lax.broadcasted_iota(jnp.int32, (rows.size, LANES), 0) + rows.start
        weight = jnp.exp(0.1 * k.astype(F32)) * (3.0 / raw_sum)
        out = []
        for scale in (None, rate_ref):
            for value in (zonal, merid):
                for half in range(2):
                    by = weight if scale is None else rate_ref[rows, HALVES[half]]
                    out.append(by * value[half])
        return out

    totals = [jnp.sum(v, axis=0, keepdims=True) for v in fourth(pl.ds(0, FREQS))]
    values = [jnp.concatenate(totals[2 * i:2 * i + 2], axis=1) * (1.0 if i < 2 else 4.0 / FREQS) for i in range(4)]
    picked = slot8.astype(F32) == slot
    lanes_of = split(jnp.concatenate([jnp.where(picked, v, 0.0) for v in values], axis=0))
    lanes_of = jnp.concatenate([lanes_of, jnp.zeros((LANES - 96, CELLS), jnp.bfloat16)], axis=0)
    table = lax.dot_general(
        from_source[:, 0:CELLS], lanes_of, (((1,), (1,)), ((), ())), preferred_element_type=F32)
    table = table + roll(table, -32) + roll(table, -64)
    back_s[...] = table.reshape(n_tile, 1, LANES)
    rows_wait(rows_s, send_sem)
    send_row(back_s, back_r, back_sem)

    def fifth(rows):
        _, _, _, _, first_y = masks(rows.size)
        for sy in range(2):
            for half in range(2):
                cut = HALVES[half]
                inner = jnp.where(first_y[sy], factor_ref[rows, cut], 0.0)
                for q in (2 * sy, 2 * sy + 1):
                    message = yr[sy, 2 + q % 2, rows, cut]
                    for j in range(NINE):
                        d = NINE * q + j
                        e0[d, rows, cut] = e0[d, rows, cut] + inner * halo_y(q, j, message)
        return ()

    each_tile(fifth)
    rows_wait(back_r, back_sem)
    rows_wait(back_s, send_sem)
    for copy in x_copy + i_copy + y_copy + c_copy + f_copy:
        copy.wait_send()


def finish(n_tile, e_ref, back_ref, route_hbm, out_hbm, coup_ref, route_in, in_sem, out_sem):
    copy = pltpu.make_async_copy(route_hbm, route_in, in_sem.at[0])
    copy.start()
    result = [
        pltpu.make_async_copy(
            e_ref.at[pl.ds(NINE * q, NINE)], out_hbm.at[pl.ds(NINE * q, NINE)], out_sem.at[q])
        for q in range(4)
    ]
    for part in result:
        part.start()
    copy.wait()
    tiles = lax.broadcasted_iota(jnp.int32, (n_tile, CELLS), 0)
    slot8 = lax.broadcasted_iota(jnp.int32, (8, CELLS), 0)
    to_dest = jnp.where(tiles == route_in[0:1], 1.0, 0.0).astype(jnp.bfloat16)
    found = gather(back_ref[...].reshape(n_tile, LANES), to_dest, 32)
    for c in range(4):
        coup_ref[c:c + 1] = jnp.sum(
            jnp.where(slot8 == route_in[1:2], found[8 * c:8 * c + 8], 0.0), axis=0, keepdims=True)
    for part in result:
        part.wait()


def solution(mesh):
    n_grp, n_tile = mesh.shape["grp"], mesh.shape["tile"]

    def body(spectrum, courant, decay, land, ice_rows, ice_route, wave_source):
        vmem = pltpu.VMEM
        dma = pltpu.SemaphoreType.DMA
        scratch = [
            vmem((DIRS, FREQS, CELLS), F32),
            vmem((1, FREQS), F32), vmem((1, FREQS), F32), vmem((SIDE, SIDE), jnp.int32),
            vmem((3, CELLS), F32), vmem((2, CELLS), jnp.int32), vmem((2, SIDE, SIDE), jnp.int32),
            vmem((10, 8, LANES), F32),
            vmem((FREQS, LANES), F32), vmem((FREQS, LANES), F32),
            vmem((FREQS, CELLS), F32), vmem((FREQS, CELLS), F32),
            vmem((FREQS, CELLS), F32), vmem((FREQS, CELLS), F32),
            vmem((2, 6, FREQS, LANES), F32), vmem((2, 6, FREQS, LANES), F32),
            vmem((2, 8, LANES), F32), vmem((2, 8, LANES), F32),
            vmem((2, 4, FREQS, CELLS), F32), vmem((2, 4, FREQS, CELLS), F32),
            vmem((4, 3, FREQS, LANES), F32), vmem((4, 3, FREQS, LANES), F32),
            vmem((2, 8, CELLS), F32), vmem((2, 8, CELLS), F32),
            vmem((n_tile, 1, LANES), F32), vmem((n_tile, 1, LANES), F32), vmem((n_tile, 1, LANES), F32),
            dma((6,)), dma((4,)), dma((13,)), dma((2,)), dma((2,)), dma((2,)), dma((4,)), dma((2,)),
            dma((1,)), dma((1,)),
        ]
        anywhere = pl.BlockSpec(memory_space=pl.ANY)
        held = pl.BlockSpec(memory_space=pltpu.VMEM)
        energy, back = pl.pallas_call(
            functools.partial(kernel, n_grp, n_tile),
            out_shape=(pltpu.VMEM((DIRS, FREQS, CELLS), F32), pltpu.VMEM((n_tile, 1, LANES), F32)),
            in_specs=[anywhere] * 7,
            out_specs=(held, held),
            scratch_shapes=scratch,
            name="coupling_step",
            compiler_params=pltpu.CompilerParams(
                collective_id=0, has_side_effects=True, vmem_limit_bytes=60 * 1024 * 1024),
        )(spectrum, courant.reshape(1, FREQS), decay.reshape(1, FREQS), land, ice_rows, ice_route, wave_source)
        return pl.pallas_call(
            functools.partial(finish, n_tile),
            out_shape=(
                jax.ShapeDtypeStruct((DIRS, FREQS, CELLS), F32),
                jax.ShapeDtypeStruct((4, CELLS), F32),
            ),
            in_specs=[held, held, anywhere],
            out_specs=(anywhere, held),
            scratch_shapes=[vmem((2, CELLS), jnp.int32), dma((1,)), dma((4,))],
            name="coupling_finish",
            compiler_params=pltpu.CompilerParams(vmem_limit_bytes=8 * 1024 * 1024),
        )(energy, back, ice_route)

    in_specs = (
        P(None, None, ("grp", "tile")),
        P(),
        P(),
        P("tile", "grp"),
        P(None, ("grp", "tile")),
        P(None, ("grp", "tile")),
        P(None, "tile", "grp"),
    )
    out_specs = (P(None, None, ("grp", "tile")), P(None, ("grp", "tile")))
    return jax.shard_map(body, mesh=mesh, in_specs=in_specs, out_specs=out_specs, check_vma=False)
```
